256 devices in a mesh: region: 32 (over x, y, core), vel: 8 (over z).
Axes of the slice: x: 4, y: 4, z: 8, core: 2. Of those that a mesh axis runs over, the one named last changes fastest.
Arguments:
- distribution: float32 [32, 8192, 384], P('region', 'vel'), may hold values from 0.05 to 2
- velocity: float32 [32, 3, 8192], P('region', None, 'vel'), may hold values from 0.3 to 6
- weights: float32 [32, 8192], P('region', 'vel'), may hold values from 0.012207031 to 0.048828125
- grid_points: int32 [32], replicated, may hold values from 1024 to 8192, as said below
- neighbours: int32 [32, 5], replicated, may hold values from 0 to 31, as said below
- interface_cells: int32 [32, 5, 16], P('region'), may hold values from 0 to 383
- interpolation: float32 [32, 5, 8192, 128], P('region', None, 'vel'), may hold values from 0 to 1
- block_inverse: float32 [32, 64, 384, 384], P('region', 'vel'), may hold values from 0 to 1
Outputs:
- updated: float32 [32, 8192, 384], P('region', 'vel')
The draws below stay inside these ranges and needn't reach their ends.
Inputs may be any that keep to these rules, and one draw needn't show every extreme that they name: `grid_points`: multiples of 128; one region has exactly 8192 points and another exactly the least. Row r lists r + 1, r - 1, r + B, r - B and r + 16, all modulo 32, for one offset B of 2 to 15 drawn anew in each draw; so every region is listed by each of its neighbours.
All inputs are finite; a program needn't handle non-finite values.
Results may differ from the reference program's by a relative error of at most 0.0003.
Values sent between devices are 32-bit elements; how exact they have to be, the bound alone decides.
A program may use at most 64 MiB of HBM per device.

```python
import math
import jax
import jax.numpy as jnp
from jax import lax

VMAX = 8192
BLK = 128
C = 384
EDGE = 16
NBR = 5
ITERS = 2
REGIONS = 32


def draw_grid_points(key, part):
    key = jax.random.fold_in(key, 3)
    first, second = jax.random.split(key)
    least = VMAX // (8 * BLK)
    sizes = BLK * jax.random.randint(first, (REGIONS,), least, VMAX // BLK + 1, dtype=jnp.int32)
    order = jax.random.permutation(second, REGIONS)
    sizes = sizes.at[order[0]].set(VMAX)
    return sizes.at[order[1]].set(BLK * least)


def draw_neighbours(key, part):
    key = jax.random.fold_in(key, 5)
    stride = jax.random.randint(key, (), 2, REGIONS // 2, dtype=jnp.int32)
    fixed = jnp.array([1, -1, 0, 0, REGIONS // 2], dtype=jnp.int32)
    signs = jnp.array([0, 0, 1, -1, 0], dtype=jnp.int32)
    regions = jnp.arange(REGIONS, dtype=jnp.int32)
    return jnp.mod(regions[:, None] + fixed[None, :] + signs[None, :] * stride, REGIONS).astype(jnp.int32)


def draw_interpolation(key, part):
    key = jax.random.fold_in(key, 7)
    first, second = jax.random.split(key)
    spread = jax.random.uniform(first, (REGIONS, NBR, VMAX, BLK), jnp.float32, 0.0, 0.8 / BLK)
    diagonal = jax.random.uniform(second, (REGIONS, NBR, VMAX), jnp.float32, 0.3, 0.7)
    within = jnp.arange(VMAX, dtype=jnp.int32) % BLK
    identity = (within[:, None] == jnp.arange(BLK, dtype=jnp.int32)[None, :]).astype(jnp.float32)
    return spread + diagonal[..., None] * identity[None, None]


def draw_block_inverse(key, part):
    key = jax.random.fold_in(key, 9)
    first, second = jax.random.split(key)
    spread = jax.random.uniform(first, (REGIONS, VMAX // BLK, C, C), jnp.float32, 0.0, 0.6 / C)
    diagonal = jax.random.uniform(second, (REGIONS, VMAX // BLK, C), jnp.float32, 0.4, 0.9)
    identity = jnp.eye(C, dtype=jnp.float32)
    return spread + diagonal[..., None] * identity[None, None]


def place_ends(values, own_key, smallest, high):
    longest = values.shape.index(max(values.shape))
    spots = []
    for shift in (0, 1):
        where = [jax.random.randint(jax.random.fold_in(own_key, axis), (), 0, length) for axis, length in enumerate(values.shape)]
        where[longest] = (where[longest] + shift) % values.shape[longest]
        spots.append(tuple(where))
    return values.at[spots[0]].set(smallest).at[spots[1]].set(high)


def level_of(key, shape, cuts, low, high):
    def one(position, parts):
        draws = jax.random.uniform(jax.random.fold_in(jax.random.fold_in(key, 6), position), (parts,), jnp.float32, low / len(cuts), high / len(cuts))
        return jnp.repeat(jnp.exp(draws), shape[position] // parts).reshape((-1,) + (1,) * (len(shape) - position - 1))

    factor_of = one(*cuts[0])
    for cut in cuts[1:]:
        factor_of = factor_of * one(*cut)
    return factor_of


def setup_inputs(seed: int = 0) -> dict:
    key_of = jax.random.split(jax.random.key(seed), 9)
    return {
        "distribution": jnp.clip(jnp.exp(math.log(2.0) - 3.6888794 * jax.random.uniform(key_of[0], (REGIONS, VMAX, C), jnp.float32) ** level_of(key_of[0], (REGIONS, VMAX, C), ((0, 32), (1, 8)), -0.2, 0.2)), 0.05, 2.0),
        "velocity": jnp.clip(jnp.exp(math.log(6.0) - 2.9957322 * jax.random.uniform(key_of[1], (REGIONS, 3, VMAX), jnp.float32) ** level_of(key_of[1], (REGIONS, 3, VMAX), ((0, 32), (2, 8)), -0.2, 0.2)), 0.3, 6.0),
        "weights": jnp.clip(jnp.exp(math.log(0.048828125) - 1.3862944 * jax.random.uniform(key_of[2], (REGIONS, VMAX), jnp.float32) ** level_of(key_of[2], (REGIONS, VMAX), ((0, 32), (1, 8)), -0.2, 0.2)), 0.012207031, 0.048828125),
        "grid_points": draw_grid_points(jax.random.fold_in(key_of[8], 71), 0),
        "neighbours": draw_neighbours(jax.random.fold_in(key_of[8], 71), 0),
        "interface_cells": place_ends(jax.random.randint(key_of[5], (REGIONS, NBR, EDGE), 0, C), jax.random.fold_in(key_of[5], 1), 0, C - 1).astype(jnp.int32),
        "interpolation": draw_interpolation(jax.random.fold_in(key_of[8], 71), 0),
        "block_inverse": draw_block_inverse(jax.random.fold_in(key_of[8], 71), 0),
    }


relax_step = 0.5
inflow_step = 0.5
viscous_conductive_ratio = 2.0 / 3.0
highest = lax.Precision.HIGHEST


def moment_basis(points):
    point_x, point_y, point_z = points[0], points[1], points[2]
    speed_sq = point_x * point_x + point_y * point_y + point_z * point_z
    return jnp.stack([jnp.ones_like(point_x), point_x, point_y, point_z,
                      point_x * point_x, point_y * point_y, point_z * point_z,
                      point_x * point_y, point_x * point_z, point_y * point_z,
                      point_x * speed_sq, point_y * speed_sq, point_z * speed_sq])


def cell_values(moments):
    particle_concentration = moments[0]
    mean_flow_first_axis = moments[1] / particle_concentration
    mean_flow_second_axis = moments[2] / particle_concentration
    mean_flow_third_axis = moments[3] / particle_concentration
    internal_agitation_content = moments[4] + moments[5] + moments[6]
    mean_flow_magnitude_sq = mean_flow_first_axis * mean_flow_first_axis + mean_flow_second_axis * mean_flow_second_axis + mean_flow_third_axis * mean_flow_third_axis
    kinetic_warmth_level = (internal_agitation_content / particle_concentration - mean_flow_magnitude_sq) / 3.0
    stress_x = moments[4] * mean_flow_first_axis + moments[7] * mean_flow_second_axis + moments[8] * mean_flow_third_axis
    stress_y = moments[7] * mean_flow_first_axis + moments[5] * mean_flow_second_axis + moments[9] * mean_flow_third_axis
    stress_z = moments[8] * mean_flow_first_axis + moments[9] * mean_flow_second_axis + moments[6] * mean_flow_third_axis
    drift = 2.0 * particle_concentration * mean_flow_magnitude_sq
    conduction_first_axis = 0.5 * (moments[10] - 2.0 * stress_x - mean_flow_first_axis * internal_agitation_content + drift * mean_flow_first_axis)
    conduction_second_axis = 0.5 * (moments[11] - 2.0 * stress_y - mean_flow_second_axis * internal_agitation_content + drift * mean_flow_second_axis)
    conduction_third_axis = 0.5 * (moments[12] - 2.0 * stress_z - mean_flow_third_axis * internal_agitation_content + drift * mean_flow_third_axis)
    return jnp.stack([particle_concentration, mean_flow_first_axis, mean_flow_second_axis, mean_flow_third_axis, kinetic_warmth_level, conduction_first_axis, conduction_second_axis, conduction_third_axis])


def shakhov(desired_outcome_list, points):
    particle_concentration = desired_outcome_list[0][None, :]
    kinetic_warmth_level = desired_outcome_list[4][None, :]
    offset_x = points[0][:, None] - desired_outcome_list[1][None, :]
    offset_y = points[1][:, None] - desired_outcome_list[2][None, :]
    offset_z = points[2][:, None] - desired_outcome_list[3][None, :]
    relative_motion_magnitude_sq = offset_x * offset_x + offset_y * offset_y + offset_z * offset_z
    stress_tensor_entry = offset_x * desired_outcome_list[5][None, :] + offset_y * desired_outcome_list[6][None, :] + offset_z * desired_outcome_list[7][None, :]
    equilibrium_prefactor = particle_concentration / (2.0 * math.pi * kinetic_warmth_level) ** 1.5
    skewed_equilibrium_adjust = 1.0 + (1.0 - viscous_conductive_ratio) * stress_tensor_entry * (relative_motion_magnitude_sq / kinetic_warmth_level - 5.0) / (5.0 * particle_concentration * kinetic_warmth_level * kinetic_warmth_level)
    return equilibrium_prefactor * jnp.exp(-relative_motion_magnitude_sq / (2.0 * kinetic_warmth_level)) * skewed_equilibrium_adjust


def gather_edges(present, edge_cells):
    neighbour_count, edge_width = edge_cells.shape
    picked = jnp.take(present, edge_cells.reshape(-1), axis=1)
    return picked.T.reshape(neighbour_count, edge_width, present.shape[0])


def interpolate_land(received, matrices, edge_cells, cell_count):
    neighbour_count, edge_width, local_points = received.shape
    block_size = matrices.shape[-1]
    block_count = local_points // block_size
    pieces = received.reshape(neighbour_count, edge_width, block_count, block_size)
    blocks = matrices.reshape(neighbour_count, block_count, block_size, block_size)
    inflow = jnp.einsum('kinu,knvu->kinv', pieces, blocks, precision=highest)
    inflow = inflow.reshape(neighbour_count * edge_width, local_points)
    onehot = (edge_cells.reshape(-1)[:, None] == jnp.arange(cell_count, dtype=jnp.int32)[None, :]).astype(jnp.float32)
    return jnp.dot(inflow.T, onehot, precision=highest)


def apply_inverse(rhs, inverse, active):
    local_points, cell_count = rhs.shape
    block_count = inverse.shape[0]
    shaped = rhs.reshape(block_count, local_points // block_count, cell_count)
    result = jnp.einsum('nvd,ncd->nvc', shaped, inverse, precision=highest)
    return result.reshape(local_points, cell_count) * active[:, None]


def reference(distribution, velocity, weights, grid_points, neighbours, interface_cells, interpolation, block_inverse):
    points = jnp.arange(VMAX, dtype=jnp.int32)
    active = (points[None, :] < grid_points[:, None]).astype(jnp.float32)
    scale = jnp.float32(VMAX) / grid_points.astype(jnp.float32)
    quad = weights * scale[:, None] * active
    start = distribution * active[:, :, None]
    partners = neighbours[neighbours]
    regions = jnp.arange(REGIONS, dtype=jnp.int32)
    slots = jnp.arange(NBR, dtype=jnp.int32)
    back = jnp.sum((partners == regions[:, None, None]).astype(jnp.int32) * slots[None, None, :], axis=-1)

    def region_update(items):
        begin, present, region_points, region_quad, region_active, edge_cells, matrices, inverse, received = items
        basis = moment_basis(region_points) * region_quad[None, :]
        moments = jnp.dot(basis, present, precision=highest)
        equilibrium = shakhov(cell_values(moments), region_points)
        landing = interpolate_land(received, matrices, edge_cells, C)
        rhs = begin + relax_step * equilibrium + inflow_step * landing
        return apply_inverse(rhs, inverse, region_active)

    current = start
    for iteration in range(ITERS):
        sent = jax.vmap(gather_edges)(current, interface_cells)
        received_all = sent[neighbours, back]
        current = lax.map(region_update, (start, current, velocity, quad, active, interface_cells,
                                          interpolation, block_inverse, received_all))
    return current
```

```python
import functools
import math

import jax
import jax.numpy as jnp
from jax import lax
from jax.experimental import pallas as pl
from jax.experimental.pallas import tpu as pltpu
from jax.sharding import PartitionSpec as P

VMAX = 8192
BLK = 128
EDGE = 16
NBR = 5
ITERS = 2
PAD = 128
BASIS = 16

relax_step = 0.5
inflow_step = 0.5
viscous_conductive_ratio = 2.0 / 3.0

MESH = pl.DeviceIdType.MESH
f32 = jnp.float32
bf16 = jnp.bfloat16


def across(a, b):
    return lax.dot_general(a, b, (((1,), (1,)), ((), ())), preferred_element_type=f32)


def plain(a, b):
    return jnp.dot(a, b, preferred_element_type=f32)


def halves(x):
    high = x.astype(bf16)
    return high, (x - high.astype(f32)).astype(bf16)


def moment_rows(x, y, z):
    speed_sq = x * x + y * y + z * z
    return [
        jnp.ones_like(x), x, y, z,
        x * x, y * y, z * z,
        x * y, x * z, y * z,
        x * speed_sq, y * speed_sq, z * speed_sq,
    ]


def cell_rows(moments):
    m = [moments[i : i + 1, :] for i in range(13)]
    density = m[0]
    over = 1.0 / density
    u, v, w = m[1] * over, m[2] * over, m[3] * over
    energy = m[4] + m[5] + m[6]
    flow_sq = u * u + v * v + w * w
    warmth = (energy * over - flow_sq) / 3.0
    stress_x = m[4] * u + m[7] * v + m[8] * w
    stress_y = m[7] * u + m[5] * v + m[9] * w
    stress_z = m[8] * u + m[9] * v + m[6] * w
    drift = 2.0 * density * flow_sq
    heat_x = 0.5 * (m[10] - 2.0 * stress_x - u * energy + drift * u)
    heat_y = 0.5 * (m[11] - 2.0 * stress_y - v * energy + drift * v)
    heat_z = 0.5 * (m[12] - 2.0 * stress_z - w * energy + drift * w)
    hot = 2.0 * math.pi * warmth
    front = relax_step * density / (hot * jnp.sqrt(hot))
    fall = -0.5 / warmth
    skew = (-2.0 * (1.0 - viscous_conductive_ratio)) / (5.0 * density * warmth * warmth)
    return [front, u, v, w, fall, heat_x * skew, heat_y * skew, heat_z * skew]


def kernel(
    stride, regions, shards, unroll,
    dist_hbm, vel_hbm, weights_hbm, points, cells, interp_hbm, inv_hbm, out_hbm,
    dist, vel, weights, interp, inv, inv_h, inv_l, edge_h, edge_l, mat_h, mat_l,
    basis_f, basis, columns, onehot_f, onehot, spread, scatter, sent, recv, part, gathered, coef, rhs, result,
    in_sem, out_sem, edge_send, edge_recv, mom_send, mom_recv,
):
    region = lax.axis_index("region")
    shard = lax.axis_index("vel")
    local, cell_count = dist.shape
    blocks = local // BLK
    width = NBR * EDGE

    loads = [
        pltpu.make_async_copy(source, target, in_sem.at[i])
        for i, (source, target) in enumerate(
            [
                (vel_hbm.at[0], vel.at[0:3]),
                (weights_hbm, weights),
                (dist_hbm.at[0], dist),
                (inv_hbm.at[0], inv),
                (interp_hbm.at[0], interp),
            ]
        )
    ]
    for load in loads:
        load.start()

    offsets = (1, regions - 1, stride, regions - stride, regions // 2)
    targets = [lax.rem(region + offset, regions) for offset in offsets]
    peers = [lax.rem(shard + step, shards) for step in range(1, shards)]
    barrier = pltpu.get_barrier_semaphore()
    for target in targets:
        pl.semaphore_signal(barrier, inc=1, device_id=(target, shard), device_id_type=MESH)
    for peer in peers:
        pl.semaphore_signal(barrier, inc=1, device_id=(region, peer), device_id_type=MESH)

    back = (1, 0, 3, 2, 4)

    def edge_copies(turn):
        return [
            pltpu.make_async_remote_copy(
                src_ref=sent.at[turn, pl.ds(EDGE * k, EDGE)],
                dst_ref=recv.at[turn, back[k]],
                send_sem=edge_send.at[turn, k],
                recv_sem=edge_recv.at[turn, back[k]],
                device_id=(targets[k], shard),
                device_id_type=MESH,
            )
            for k in range(NBR)
        ]

    def moment_copies(turn):
        return [
            pltpu.make_async_remote_copy(
                src_ref=part.at[turn],
                dst_ref=gathered.at[turn, j],
                send_sem=mom_send.at[turn, j],
                recv_sem=mom_recv.at[turn, j],
                device_id=(region, peers[j]),
                device_id_type=MESH,
            )
            for j in range(shards - 1)
        ]

    total = points[region]

    def alive(n):
        return jnp.where((shard * blocks + n) * BLK < total, f32(1.0), f32(0.0))

    def rows_of(n):
        return pl.ds(pl.multiple_of(n * BLK, BLK), BLK)

    def each(body, init=0):
        return lax.fori_loop(0, blocks, body, init, unroll=unroll)

    vel[3:8, :] = jnp.zeros((5, local), f32)
    onehot_f[...] = jnp.zeros_like(onehot_f)
    lane = lax.broadcasted_iota(jnp.int32, (1, cell_count), 1)
    for k in range(NBR):
        for i in range(EDGE):
            row = EDGE * k + i
            onehot_f[row : row + 1, :] = (lane == cells[0, k, i]).astype(f32)
    picks = onehot_f[...]
    onehot[...] = picks.astype(bf16)
    halved = (inflow_step * picks).astype(bf16)
    spread[0:PAD, :] = halved
    spread[PAD : 2 * PAD, :] = halved

    loads[0].wait()
    loads[1].wait()
    x, y, z = vel[0:1, :], vel[1:2, :], vel[2:3, :]
    place = shard * local + lax.broadcasted_iota(jnp.int32, (1, local), 1)
    scale = f32(VMAX) / jnp.full((1, local), total.astype(f32))
    quad = weights[...] * scale * (place < total).astype(f32)
    basis_f[...] = jnp.zeros_like(basis_f)
    for i, row in enumerate(moment_rows(x, y, z)):
        basis_f[i : i + 1, :] = row * quad

    def split_basis(n, carry):
        high, low = halves(basis_f[:, rows_of(n)])
        basis[n, 0:BASIS] = high
        basis[n, BASIS : 2 * BASIS] = low
        return carry

    each(split_basis)

    loads[2].wait()

    def first_moments(n, acc):
        high, low = halves(dist[rows_of(n), :] * alive(n))
        both = plain(basis[n], high)
        return acc + both[:BASIS] + both[BASIS:] + plain(basis[n, 0:BASIS], low)

    part[0] = each(first_moments, jnp.zeros((BASIS, cell_count), f32))
    pl.semaphore_wait(barrier, NBR + shards - 1)
    moments_out = [moment_copies(0), moment_copies(1)]
    edges_out = [edge_copies(0), edge_copies(1)]
    for copy in moments_out[0]:
        copy.start()

    def first_edges(n, carry):
        high, low = halves(dist[rows_of(n), :] * alive(n))
        pick = onehot[0:width]
        sent[0, :, rows_of(n)] = across(pick, high) + across(pick, low)
        return carry

    each(first_edges)
    for copy in edges_out[0]:
        copy.start()

    scatter[...] = jnp.zeros_like(scatter)
    loads[3].wait()
    loads[4].wait()

    def prepare(n, carry):
        high, low = halves(inv[n])
        inv_h[n] = high
        inv_l[n] = low
        pick = onehot[0:width]
        edge_h[n] = plain(pick, high).astype(bf16)
        edge_l[n] = plain(pick, low).astype(bf16)
        for k in range(NBR):
            high, low = halves(interp[k, rows_of(n), :])
            mat_h[n, :, BLK * k : BLK * (k + 1)] = high
            mat_l[n, :, BLK * k : BLK * (k + 1)] = low
        turned = jnp.transpose(vel[:, rows_of(n)])
        for axis in range(3):
            columns[axis, rows_of(n), :] = jnp.broadcast_to(turned[:, axis : axis + 1], (BLK, 128))
        return carry

    each(prepare)

    def collect(turn):
        for copy in moments_out[turn]:
            copy.wait_recv()
        moments = part[turn]
        for j in range(shards - 1):
            moments = moments + gathered[turn, j]
        for i, row in enumerate(cell_rows(moments)):
            coef[i : i + 1, :] = row

    def relax(n, carry):
        on = alive(n)
        chunk = 32
        for tile in range(cell_count // 128):
            lanes = pl.ds(128 * tile, 128)
            front, u, v, w, fall, skew_x, skew_y, skew_z = [coef[i : i + 1, lanes] for i in range(8)]
            for c in range(BLK // chunk):
                rows = pl.ds(pl.multiple_of(n * BLK + c * chunk, chunk), chunk)
                e_x = columns[0, rows, :] - u
                e_y = columns[1, rows, :] - v
                e_z = columns[2, rows, :] - w
                power = (e_x * e_x + e_y * e_y + e_z * e_z) * fall
                lean = e_x * skew_x + e_y * skew_y + e_z * skew_z
                value = front * jnp.exp(power) * (1.0 + lean * (power + 2.5))
                rhs[rows, lanes] = dist[rows, lanes] * on + value
        return carry

    def arrive(turn):
        for k in range(NBR):
            edges_out[turn][back[k]].wait_recv()
            for n in range(blocks):
                high, low = halves(recv[turn, k, :, BLK * n : BLK * (n + 1)])
                lanes = slice(BLK * k, BLK * (k + 1))
                scatter[n, EDGE * k : EDGE * (k + 1), lanes] = high
                scatter[n, PAD + EDGE * k : PAD + EDGE * (k + 1), lanes] = low

    def landed(n):
        wide = across(mat_h[n], scatter[n])
        inflow = wide[:, :PAD] + wide[:, PAD:] + across(mat_l[n], scatter[n, 0:PAD])
        high, low = halves(inflow)
        return rhs[rows_of(n), :] + plain(jnp.concatenate([high, low], axis=1), spread[...])

    collect(0)
    each(relax)
    arrive(0)

    def middle(n, acc):
        high, low = halves(landed(n))
        edges = across(edge_h[n], high) + across(edge_h[n], low) + across(edge_l[n], high)
        sent[1, :, rows_of(n)] = edges * alive(n)
        both = plain(basis[n], high)
        held = both[:BASIS] + both[BASIS:] + plain(basis[n, 0:BASIS], low)
        held_h, held_l = halves(held)
        both = across(jnp.concatenate([held_h, held_l], axis=0), inv_h[n])
        return acc + both[:BASIS] + both[BASIS:] + across(held_h, inv_l[n])

    part[1] = each(middle, jnp.zeros((BASIS, cell_count), f32))
    for copy in moments_out[1]:
        copy.start()
    for copy in edges_out[1]:
        copy.start()
    collect(1)
    each(relax)
    arrive(1)

    def last(n, carry):
        high, low = halves(landed(n))
        value = across(high, inv_h[n]) + across(low, inv_h[n]) + across(high, inv_l[n])
        result[rows_of(n), :] = value * alive(n)
        pltpu.make_async_copy(result.at[rows_of(n)], out_hbm.at[0, rows_of(n)], out_sem.at[n]).start()
        return carry

    each(last)
    for n in range(blocks):
        rows = pl.ds(n * BLK, BLK)
        pltpu.make_async_copy(result.at[rows], out_hbm.at[0, rows], out_sem.at[n]).wait()
    for turn in range(ITERS):
        for copy in moments_out[turn] + edges_out[turn]:
            copy.wait_send()


def update(stride, regions, shards, unroll, *arrays):
    distribution, velocity, weights, points, cells, interpolation, inverse = arrays
    local, cell_count = distribution.shape[1:]
    blocks = local // BLK
    width = NBR * EDGE
    anywhere = pl.BlockSpec(memory_space=pl.ANY)
    scalars = pl.BlockSpec(memory_space=pltpu.SMEM)
    vmem = pltpu.VMEM
    return pl.pallas_call(
        functools.partial(kernel, stride, regions, shards, unroll),
        out_shape=jax.ShapeDtypeStruct((1, local, cell_count), f32),
        in_specs=[anywhere, anywhere, anywhere, scalars, scalars, anywhere, anywhere],
        out_specs=anywhere,
        scratch_shapes=[
            vmem((local, cell_count), f32),
            vmem((8, local), f32),
            vmem((1, local), f32),
            vmem((NBR, local, BLK), f32),
            vmem((blocks, cell_count, cell_count), f32),
            vmem((blocks, cell_count, cell_count), bf16),
            vmem((blocks, cell_count, cell_count), bf16),
            vmem((blocks, width, cell_count), bf16),
            vmem((blocks, width, cell_count), bf16),
            vmem((blocks, BLK, NBR * BLK), bf16),
            vmem((blocks, BLK, NBR * BLK), bf16),
            vmem((BASIS, local), f32),
            vmem((blocks, 2 * BASIS, BLK), bf16),
            vmem((3, local, 128), f32),
            vmem((PAD, cell_count), f32),
            vmem((PAD, cell_count), bf16),
            vmem((2 * PAD, cell_count), bf16),
            vmem((blocks, 2 * PAD, NBR * BLK), bf16),
            vmem((ITERS, width, local), f32),
            vmem((ITERS, NBR, EDGE, local), f32),
            vmem((ITERS, BASIS, cell_count), f32),
            vmem((ITERS, shards - 1, BASIS, cell_count), f32),
            vmem((8, cell_count), f32),
            vmem((local, cell_count), f32),
            vmem((local, cell_count), f32),
            pltpu.SemaphoreType.DMA((5,)),
            pltpu.SemaphoreType.DMA((blocks,)),
            pltpu.SemaphoreType.DMA((ITERS, NBR)),
            pltpu.SemaphoreType.DMA((ITERS, NBR)),
            pltpu.SemaphoreType.DMA((ITERS, shards - 1)),
            pltpu.SemaphoreType.DMA((ITERS, shards - 1)),
        ],
        compiler_params=pltpu.CompilerParams(
            collective_id=stride, has_side_effects=True, vmem_limit_bytes=56 * 1024 * 1024
        ),
    )(distribution, velocity, weights, points, cells, interpolation, inverse)


def solution(mesh):
    regions, shards = mesh.shape["region"], mesh.shape["vel"]
    strides = range(2, regions // 2)

    def local(distribution, velocity, weights, grid_points, neighbours, interface_cells, interpolation, block_inverse):
        stride = jnp.mod(neighbours[0, 2], regions)
        branches = [functools.partial(update, s, regions, shards, 1) for s in strides]
        return lax.switch(
            stride - strides[0], branches,
            distribution, velocity, weights, grid_points, interface_cells, interpolation, block_inverse,
        )

    placed = (
        P("region", "vel", None),
        P("region", None, "vel"),
        P("region", "vel"),
        P(),
        P(),
        P("region", None, None),
        P("region", None, "vel", None),
        P("region", "vel", None, None),
    )
    return jax.shard_map(
        local, mesh=mesh, in_specs=placed, out_specs=P("region", "vel", None), check_vma=False
    )
```

```python
import functools
import math

import jax
import jax.numpy as jnp
from jax import lax
from jax.experimental import pallas as pl
from jax.experimental.pallas import tpu as pltpu
from jax.sharding import PartitionSpec as P

VMAX = 8192
BLK = 128
EDGE = 16
NBR = 5
ITERS = 2
PAD = 128
WIDE = 256
BASIS = 16
TILE = 8

relax_step = 0.5
inflow_step = 0.5
viscous_conductive_ratio = 2.0 / 3.0

MESH = pl.DeviceIdType.MESH
f32 = jnp.float32
bf16 = jnp.bfloat16


def across(a, b):
    return lax.dot_general(a, b, (((1,), (1,)), ((), ())), preferred_element_type=f32)


def plain(a, b):
    return jnp.dot(a, b, preferred_element_type=f32)


def halves(x):
    high = x.astype(bf16)
    return high, (x - high.astype(f32)).astype(bf16)


def moment_rows(x, y, z):
    speed_sq = x * x + y * y + z * z
    return [
        jnp.ones_like(x), x, y, z,
        x * x, y * y, z * z,
        x * y, x * z, y * z,
        x * speed_sq, y * speed_sq, z * speed_sq,
    ]


def cell_rows(m):
    density = m[0]
    over = 1.0 / density
    u, v, w = m[1] * over, m[2] * over, m[3] * over
    energy = m[4] + m[5] + m[6]
    flow_sq = u * u + v * v + w * w
    warmth = (energy * over - flow_sq) / 3.0
    stress_x = m[4] * u + m[7] * v + m[8] * w
    stress_y = m[7] * u + m[5] * v + m[9] * w
    stress_z = m[8] * u + m[9] * v + m[6] * w
    drift = 2.0 * density * flow_sq
    heat_x = 0.5 * (m[10] - 2.0 * stress_x - u * energy + drift * u)
    heat_y = 0.5 * (m[11] - 2.0 * stress_y - v * energy + drift * v)
    heat_z = 0.5 * (m[12] - 2.0 * stress_z - w * energy + drift * w)
    hot = 2.0 * math.pi * warmth
    front = relax_step * density / (hot * jnp.sqrt(hot))
    fall = -0.5 / warmth
    skew = (-2.0 * (1.0 - viscous_conductive_ratio)) / (5.0 * density * warmth * warmth)
    return [front, u, v, w, fall, heat_x * skew, heat_y * skew, heat_z * skew]


def kernel(
    regions, shards, unroll,
    dist_hbm, vel_hbm, weights_hbm, points, neighbours, cells, interp_hbm, inv_hbm, out_hbm,
    dist, vel, weights, interp, inv, both_inv, both_edge, edge_edge, inv_edge, mats,
    basis_f, basis, columns, onehot_f, onehot, halved, pieces, flow_t, flow, kept, sent, recv, tiles, hold_a, hold_b, moved, reached, part, gathered, coef, rhs, result,
    in_sem, out_sem, edge_send, edge_recv, hop_send, hop_recv, part_send, part_recv,
):
    region = lax.axis_index("region")
    shard = lax.axis_index("vel")
    local, cell_count = dist.shape
    blocks = local // BLK
    width = NBR * EDGE

    loads = [
        pltpu.make_async_copy(source, target, in_sem.at[i])
        for i, (source, target) in enumerate(
            [
                (dist_hbm.at[0], dist),
                (vel_hbm, vel),
                (weights_hbm, weights),
                (inv_hbm.at[0], inv),
                (interp_hbm.at[0], interp),
            ]
        )
    ]
    for load in loads:
        load.start()

    def shifted(offset):
        return lax.rem(region + offset + regions, regions)

    peers = [lax.rem(shard + step, shards) for step in range(1, shards)]
    barrier = pltpu.get_barrier_semaphore()

    def others(body):
        def one(offset, carry):
            body(shifted(offset))
            return carry

        lax.fori_loop(1, regions, one, 0)

    others(lambda r: pl.semaphore_signal(barrier, inc=1, device_id=(r, shard), device_id_type=MESH))
    for peer in peers:
        pl.semaphore_signal(barrier, inc=1, device_id=(region, peer), device_id_type=MESH)

    def remote(source, target, send, arrive, device):
        return pltpu.make_async_remote_copy(
            src_ref=source, dst_ref=target, send_sem=send, recv_sem=arrive, device_id=device, device_id_type=MESH
        )

    def slot_rows(k):
        return pl.ds(EDGE * k, EDGE)

    direct_copies = [
        [
            remote(
                sent.at[turn, slot_rows(k)], recv.at[turn, j], edge_send.at[turn, j], edge_recv.at[turn, j],
                (shifted(offset), shard),
            )
            for j, (k, offset) in enumerate(((1, -1), (0, 1), (4, regions // 2)))
        ]
        for turn in range(ITERS)
    ]
    hold = (hold_a, hold_b)

    def out_copy(turn, r):
        return remote(tiles.at[turn, r], hold[turn].at[region], hop_send.at[turn, 0], hop_recv.at[turn, 0], (r, shard))

    def on_copy(turn, r):
        return remote(moved.at[turn, r], reached.at[turn, region], hop_send.at[turn, 1], hop_recv.at[turn, 1], (r, shard))

    def all_tiles(turn, step):
        ref = (hold[turn] if step == 0 else reached.at[turn]).at[pl.ds(0, regions - 1)]
        return remote(ref, ref, hop_send.at[turn, step], hop_recv.at[turn, step], (shifted(1), shard))

    part_copies = [
        [
            remote(part.at[turn], gathered.at[turn, j], part_send.at[turn, j], part_recv.at[turn, j], (region, peers[j]))
            for j in range(shards - 1)
        ]
        for turn in range(ITERS)
    ]

    total = points[region]
    stride = lax.rem(neighbours[2, 0] + regions, regions)
    backward = jnp.where(region < regions // 2, regions - stride, stride)

    def alive(n):
        return jnp.where((shard * blocks + n) * BLK < total, f32(1.0), f32(0.0))

    def rows_of(n):
        return pl.ds(pl.multiple_of(n * BLK, BLK), BLK)

    def each(body, init=0):
        return lax.fori_loop(0, blocks, body, init, unroll=unroll)

    def post_edges(turn, n, edges):
        sent[turn, :, rows_of(n)] = edges
        for group in range(regions // blocks):
            start = 2 * EDGE + TILE * group
            tiles[turn, group * blocks + n] = edges[start : start + TILE]

    def send_edges(turn):
        hold[turn][region] = tiles[turn, region]
        others(lambda r: out_copy(turn, r).start())
        for copy in direct_copies[turn]:
            copy.start()

    def send_part(turn, total_part):
        part[turn] = total_part
        for copy in part_copies[turn]:
            copy.start()

    with jax.named_scope("onehot"):
        onehot_f[...] = jnp.zeros_like(onehot_f)
        lane = lax.broadcasted_iota(jnp.int32, (1, cell_count), 1)
        for k in range(NBR):
            for i in range(EDGE):
                row = EDGE * k + i
                onehot_f[row : row + 1, :] = (lane == cells[k, 0, i]).astype(f32)
        picks = onehot_f[...]
        onehot[...] = picks.astype(bf16)
        half = (inflow_step * picks[0:width]).astype(bf16)
        halved[3 * width :, :] = jnp.zeros((WIDE - 3 * width, cell_count), bf16)
        for i in range(3):
            halved[i * width : (i + 1) * width, :] = half

    with jax.named_scope("wait_dist"):
        loads[0].wait()

    def first_edges(n, carry):
        high, low = halves(dist[rows_of(n), :] * alive(n))
        pick = onehot[0:width]
        post_edges(0, n, across(pick, high) + across(pick, low))
        return carry

    with jax.named_scope("first_edges"):
        each(first_edges)

    with jax.named_scope("entry"):
        pl.semaphore_wait(barrier, regions + shards - 2)
        send_edges(0)

    with jax.named_scope("basis"):
        loads[1].wait()
        loads[2].wait()
        x, y, z = vel[0], vel[1], vel[2]
        place = shard * local + lax.broadcasted_iota(jnp.int32, (1, local), 1)
        scale = f32(VMAX) / jnp.full((1, local), total.astype(f32))
        quad = weights[...] * scale * (place < total).astype(f32)
        basis_f[...] = jnp.zeros_like(basis_f)
        for i, row in enumerate(moment_rows(x, y, z)):
            basis_f[i : i + 1, :] = row * quad

        def split_basis(n, carry):
            high, low = halves(basis_f[:, rows_of(n)])
            basis[n, 0:BASIS, 0:BLK] = high
            basis[n, 0:BASIS, BLK : 2 * BLK] = high
            basis[n, BASIS : 2 * BASIS, 0:BLK] = low
            basis[n, BASIS : 2 * BASIS, BLK : 2 * BLK] = jnp.zeros_like(low)
            return carry

        each(split_basis)

    def weighted(n, high, low):
        both = plain(basis[n], jnp.concatenate([high, low], axis=0))
        return both[:BASIS] + both[BASIS:]

    def first_moments(n, acc):
        high, low = halves(dist[rows_of(n), :] * alive(n))
        return acc + weighted(n, high, low)

    with jax.named_scope("first_moments"):
        send_part(0, each(first_moments, jnp.zeros((BASIS, cell_count), f32)))

    with jax.named_scope("turn_columns"):
        basis_f[0:3, :] = jnp.concatenate([x, y, z], axis=0)

        def turn_columns(n, carry):
            turned = jnp.transpose(basis_f[0:8, rows_of(n)])
            for axis in range(3):
                columns[axis, rows_of(n), :] = jnp.broadcast_to(turned[:, axis : axis + 1], (BLK, 128))
            return carry

        each(turn_columns)
        pieces[...] = jnp.zeros_like(pieces)
        flow_t[...] = jnp.zeros_like(flow_t)

    def forward(turn):
        all_tiles(turn, 0).wait_recv()

        def take(r, carry):
            moved[turn, r] = hold[turn][lax.rem(r + backward, regions)]
            return carry

        lax.fori_loop(0, regions, take, 0, unroll=8)
        reached[turn, region] = moved[turn, region]
        others(lambda r: on_copy(turn, r).start())

    def prepare_inv(n, carry):
        high, low = halves(inv[n])
        both_inv[n, :, 0:cell_count] = high
        both_inv[n, :, cell_count : 2 * cell_count] = low
        edges = plain(onehot[0:width], jnp.concatenate([high, low], axis=1)).astype(bf16)
        both_edge[n, 0:width, 0:cell_count] = edges[:, 0:cell_count]
        both_edge[n, 0:width, cell_count : 2 * cell_count] = edges[:, 0:cell_count]
        both_edge[n, width : 2 * width, 0:cell_count] = edges[:, cell_count : 2 * cell_count]
        both_edge[n, width : 2 * width, cell_count : 2 * cell_count] = jnp.zeros((width, cell_count), bf16)
        back_h = across(halved[0:width], high).astype(bf16)
        inv_edge[n, 0:width] = back_h
        inv_edge[n, width : 2 * width] = back_h
        inv_edge[n, 2 * width : WIDE] = across(halved[2 * width : WIDE], low).astype(bf16)
        near = across(edges[:, 0:cell_count], halved[...])
        fine = across(edges[:, cell_count : 2 * cell_count], halved[...])
        lane = lax.broadcasted_iota(jnp.int32, (width, WIDE), 1)
        edge_edge[n] = jnp.where(lane < 2 * width, near, fine).astype(bf16)
        return carry

    def prepare_mat(n, carry):
        for k in range(NBR):
            high, low = halves(interp[k, rows_of(n), :])
            mats[n, k, :, 0:BLK] = high
            mats[n, k, :, BLK : 2 * BLK] = low
        return carry

    with jax.named_scope("prepare_inv"):
        loads[3].wait()
        each(prepare_inv)
    with jax.named_scope("forward0"):
        forward(0)
    with jax.named_scope("prepare_mat"):
        loads[4].wait()
        each(prepare_mat)

    def collect(turn):
        for copy in part_copies[turn]:
            copy.wait_recv()
        moments = part[turn]
        for j in range(shards - 1):
            moments = moments + gathered[turn, j]
        rows = cell_rows([moments[i : i + 1, :] for i in range(13)])
        for i, row in enumerate(rows):
            coef[i : i + 1, :] = row

    def relax(n, carry):
        on = alive(n)
        chunk = 32
        for tile in range(cell_count // 128):
            lanes = pl.ds(128 * tile, 128)
            front, u, v, w, fall, skew_x, skew_y, skew_z = [coef[i : i + 1, lanes] for i in range(8)]
            for c in range(BLK // chunk):
                rows = pl.ds(pl.multiple_of(n * BLK + c * chunk, chunk), chunk)
                e_x = columns[0, rows, :] - u
                e_y = columns[1, rows, :] - v
                e_z = columns[2, rows, :] - w
                power = (e_x * e_x + e_y * e_y + e_z * e_z) * fall
                lean = e_x * skew_x + e_y * skew_y + e_z * skew_z
                value = front * jnp.exp(power) * (1.0 + lean * (power + 2.5))
                rhs[rows, lanes] = dist[rows, lanes] * on + value
        return carry

    def place_in(k, value):
        high, low = halves(value)
        for n in range(blocks):
            lanes = slice(BLK * n, BLK * (n + 1))
            pieces[n, k, 0:EDGE, 0:BLK] = high[:, lanes]
            pieces[n, k, 0:EDGE, BLK : 2 * BLK] = high[:, lanes]
            pieces[n, k, EDGE : 2 * EDGE, 0:BLK] = low[:, lanes]

    def arrive(turn):
        for j, k in enumerate((0, 1, 4)):
            direct_copies[turn][j].wait_recv()
            place_in(k, recv[turn, j])
        all_tiles(turn, 1).wait_recv()
        for k, first in ((3, 0), (2, 2 * blocks)):
            rows = [[reached[turn, first + g * blocks + n] for n in range(blocks)] for g in range(2)]
            place_in(k, jnp.concatenate([jnp.concatenate(r, axis=1) for r in rows], axis=0))

    def interpolate(n, carry):
        flows = []
        for k in range(NBR):
            both = across(pieces[n, k], mats[n, k])
            flows.append(both[:EDGE] + both[EDGE:])
        high, low = halves(jnp.concatenate(flows, axis=0))
        flow_t[n, 0:width] = high
        flow_t[n, width : 2 * width] = low
        flow_t[n, 2 * width : 3 * width] = high
        flow[n] = jnp.transpose(flow_t[n])
        return carry

    with jax.named_scope("collect0"):
        collect(0)
    with jax.named_scope("relax0"):
        each(relax)

    def main_edges(n, carry):
        high, low = halves(rhs[rows_of(n), :])
        edges = across(both_edge[n], jnp.concatenate([high, low], axis=1))
        kept[n] = edges[:width] + edges[width:]
        return carry

    def main_moments(n, acc):
        high, low = halves(rhs[rows_of(n), :])
        held_h, held_l = halves(weighted(n, high, low))
        held = jnp.concatenate(
            [
                jnp.concatenate([held_h, held_h], axis=1),
                jnp.concatenate([held_l, jnp.zeros_like(held_l)], axis=1),
            ],
            axis=0,
        )
        both = across(held, both_inv[n])
        return acc + both[:BASIS] + both[BASIS:]

    with jax.named_scope("main_edges"):
        each(main_edges)
    with jax.named_scope("main_moments"):
        main_part = each(main_moments, jnp.zeros((BASIS, cell_count), f32))
    with jax.named_scope("arrive0"):
        arrive(0)
    with jax.named_scope("interpolate0"):
        each(interpolate)

    def landed_edges(n, carry):
        post_edges(1, n, (kept[n] + plain(edge_edge[n], flow_t[n])) * alive(n))
        return carry

    def landed_moments(n, acc):
        both = plain(basis[n, :, 0:BLK], flow[n])
        held_h, held_l = halves(both[:BASIS] + both[BASIS:])
        both = plain(jnp.concatenate([held_h, held_l], axis=0), inv_edge[n])
        return acc + both[:BASIS] + both[BASIS:]

    with jax.named_scope("landed_edges"):
        each(landed_edges)
        send_edges(1)
    with jax.named_scope("landed_moments"):
        send_part(1, each(landed_moments, main_part))
    with jax.named_scope("forward1"):
        forward(1)
    with jax.named_scope("collect1"):
        collect(1)
    with jax.named_scope("relax1"):
        each(relax)

    def main_result(n, carry):
        high, low = halves(rhs[rows_of(n), :])
        value = across(jnp.concatenate([high, high], axis=1), both_inv[n])
        result[rows_of(n), :] = value + across(low, both_inv[n, :, 0:cell_count])
        return carry

    def last(n, carry):
        result[rows_of(n), :] = (result[rows_of(n), :] + plain(flow[n], inv_edge[n])) * alive(n)
        pltpu.make_async_copy(result.at[rows_of(n)], out_hbm.at[0, rows_of(n)], out_sem.at[n]).start()
        return carry

    with jax.named_scope("main_result"):
        each(main_result)
    with jax.named_scope("arrive1"):
        arrive(1)
    with jax.named_scope("interpolate1"):
        each(interpolate)
    with jax.named_scope("last"):
        each(last)
    with jax.named_scope("finish"):
        for n in range(blocks):
            rows = pl.ds(n * BLK, BLK)
            pltpu.make_async_copy(result.at[rows], out_hbm.at[0, rows], out_sem.at[n]).wait()
        for turn in range(ITERS):
            for copy in part_copies[turn] + direct_copies[turn]:
                copy.wait_send()
            for step in range(2):
                all_tiles(turn, step).wait_send()


def update(regions, shards, unroll, *arrays):
    distribution, velocity, weights, points, neighbours, cells, interpolation, inverse = arrays
    local, cell_count = distribution.shape[1:]
    blocks = local // BLK
    width = NBR * EDGE
    anywhere = pl.BlockSpec(memory_space=pl.ANY)
    scalars = pl.BlockSpec(memory_space=pltpu.SMEM)
    vmem = pltpu.VMEM
    signals = pltpu.SemaphoreType.DMA
    return pl.pallas_call(
        functools.partial(kernel, regions, shards, unroll),
        out_shape=jax.ShapeDtypeStruct((1, local, cell_count), f32),
        in_specs=[anywhere, anywhere, anywhere, scalars, scalars, scalars, anywhere, anywhere],
        out_specs=anywhere,
        scratch_shapes=[
            vmem((local, cell_count), f32),
            vmem((3, 1, local), f32),
            vmem((1, local), f32),
            vmem((NBR, local, BLK), f32),
            vmem((blocks, cell_count, cell_count), f32),
            vmem((blocks, cell_count, 2 * cell_count), bf16),
            vmem((blocks, 2 * width, 2 * cell_count), bf16),
            vmem((blocks, width, WIDE), bf16),
            vmem((blocks, WIDE, cell_count), bf16),
            vmem((blocks, NBR, BLK, 2 * BLK), bf16),
            vmem((BASIS, local), f32),
            vmem((blocks, 2 * BASIS, 2 * BLK), bf16),
            vmem((3, local, 128), f32),
            vmem((PAD, cell_count), f32),
            vmem((PAD, cell_count), bf16),
            vmem((WIDE, cell_count), bf16),
            vmem((blocks, NBR, 2 * EDGE, 2 * BLK), bf16),
            vmem((blocks, WIDE, BLK), bf16),
            vmem((blocks, BLK, WIDE), bf16),
            vmem((blocks, width, BLK), f32),
            vmem((ITERS, width, local), f32),
            vmem((ITERS, 3, EDGE, local), f32),
            vmem((ITERS, regions, TILE, BLK), f32),
            vmem((regions, TILE, BLK), f32),
            vmem((regions, TILE, BLK), f32),
            vmem((ITERS, regions, TILE, BLK), f32),
            vmem((ITERS, regions, TILE, BLK), f32),
            vmem((ITERS, BASIS, cell_count), f32),
            vmem((ITERS, shards - 1, BASIS, cell_count), f32),
            vmem((8, cell_count), f32),
            vmem((local, cell_count), f32),
            vmem((local, cell_count), f32),
            signals((5,)),
            signals((blocks,)),
            signals((ITERS, 3)),
            signals((ITERS, 3)),
            signals((ITERS, 2)),
            signals((ITERS, 2)),
            signals((ITERS, shards - 1)),
            signals((ITERS, shards - 1)),
        ],
        compiler_params=pltpu.CompilerParams(
            collective_id=0, has_side_effects=True, vmem_limit_bytes=56 * 1024 * 1024
        ),
    )(distribution, velocity, weights, points, neighbours, cells, interpolation, inverse)


def solution(mesh):
    regions, shards = mesh.shape["region"], mesh.shape["vel"]

    def local(distribution, velocity, weights, grid_points, neighbours, interface_cells, interpolation, block_inverse):
        return update(
            regions, shards, 8,
            distribution, velocity.transpose(1, 0, 2), weights, grid_points, neighbours.T,
            interface_cells.transpose(1, 0, 2), interpolation, block_inverse,
        )

    placed = (
        P("region", "vel", None),
        P("region", None, "vel"),
        P("region", "vel"),
        P(),
        P(),
        P("region", None, None),
        P("region", None, "vel", None),
        P("region", "vel", None, None),
    )
    return jax.shard_map(
        local, mesh=mesh, in_specs=placed, out_specs=P("region", "vel", None), check_vma=False
    )
```

```python
import functools
import math

import jax
import jax.numpy as jnp
from jax import lax
from jax.experimental import pallas as pl
from jax.experimental.pallas import tpu as pltpu
from jax.sharding import PartitionSpec as P

VMAX = 8192
BLK = 128
EDGE = 16
NBR = 5
ITERS = 2
PAD = 128
WIDE = 256
BASIS = 16
MOMENTS = 13
TILE = 8

relax_step = 0.5
inflow_step = 0.5
viscous_conductive_ratio = 2.0 / 3.0

MESH = pl.DeviceIdType.MESH
f32 = jnp.float32
bf16 = jnp.bfloat16


def far_first(regions):
    side = math.isqrt(regions // 2)

    def hops(offset):
        total = 0
        for region in range(regions):
            here, there = region // 2, (region + offset) % regions // 2
            for a, b in ((here // side, there // side), (here % side, there % side)):
                total += min((a - b) % side, (b - a) % side)
        return total

    return sorted(range(1, regions), key=lambda offset: (-hops(offset), offset))


def across(a, b):
    return lax.dot_general(a, b, (((1,), (1,)), ((), ())), preferred_element_type=f32)


def plain(a, b):
    return jnp.dot(a, b, preferred_element_type=f32)


def halves(x):
    high = x.astype(bf16)
    return high, (x - high.astype(f32)).astype(bf16)


def moment_rows(x, y, z):
    speed_sq = x * x + y * y + z * z
    return [
        jnp.ones_like(x), x, y, z,
        x * x, y * y, z * z,
        x * y, x * z, y * z,
        x * speed_sq, y * speed_sq, z * speed_sq,
    ]


def cell_rows(m):
    density = m[0]
    over = 1.0 / density
    u, v, w = m[1] * over, m[2] * over, m[3] * over
    energy = m[4] + m[5] + m[6]
    flow_sq = u * u + v * v + w * w
    warmth = (energy * over - flow_sq) / 3.0
    stress_x = m[4] * u + m[7] * v + m[8] * w
    stress_y = m[7] * u + m[5] * v + m[9] * w
    stress_z = m[8] * u + m[9] * v + m[6] * w
    drift = 2.0 * density * flow_sq
    heat_x = 0.5 * (m[10] - 2.0 * stress_x - u * energy + drift * u)
    heat_y = 0.5 * (m[11] - 2.0 * stress_y - v * energy + drift * v)
    heat_z = 0.5 * (m[12] - 2.0 * stress_z - w * energy + drift * w)
    hot = 2.0 * math.pi * warmth
    front = relax_step * density / (hot * jnp.sqrt(hot))
    fall = -0.5 / warmth
    skew = (-2.0 * (1.0 - viscous_conductive_ratio)) / (5.0 * density * warmth * warmth)
    return [front, u, v, w, fall, heat_x * skew, heat_y * skew, heat_z * skew]


def kernel(
    regions, shards, unroll,
    dist_hbm, vel_hbm, weights_hbm, points_hbm, neighbours_hbm, cells_hbm, interp_hbm, inv_hbm, out,
    points, neighbours, cells, dist, vel, weights, interp, inv, both_inv, both_edge, edge_edge, inv_edge, mats,
    basis_f, basis, columns, onehot_f, onehot, halved, pieces, flow_t, flow, kept, sent, recv, tiles, hold_a, hold_b, moved, reached, part, gathered, coef, rhs,
    in_sem, edge_send, edge_recv, hop_send, hop_recv, part_send, part_recv,
):
    region = lax.axis_index("region")
    shard = lax.axis_index("vel")
    local, cell_count = dist.shape
    blocks = local // BLK
    width = NBR * EDGE

    def shifted(offset):
        return lax.rem(region + offset + regions, regions)

    steps = sorted(range(1, shards), key=lambda step: -min(step, shards - step))
    peers = [lax.rem(shard + step, shards) for step in steps]
    offsets = far_first(regions)
    barrier = pltpu.get_barrier_semaphore()

    def others(body):
        for offset in offsets:
            body(shifted(offset))

    for peer in peers:
        pl.semaphore_signal(barrier, inc=1, device_id=(region, peer), device_id_type=MESH)
    others(lambda r: pl.semaphore_signal(barrier, inc=1, device_id=(r, shard), device_id_type=MESH))

    loads = [
        pltpu.make_async_copy(source, target, in_sem.at[i])
        for i, (source, target) in enumerate(
            [
                (dist_hbm.at[0], dist),
                (vel_hbm, vel),
                (weights_hbm, weights),
                (inv_hbm.at[0], inv),
                (interp_hbm.at[0], interp),
                (cells_hbm, cells),
                (points_hbm, points),
                (neighbours_hbm, neighbours),
            ]
        )
    ]
    for i in (5, 6, 0, 7, 1, 2):
        loads[i].start()

    def remote(source, target, send, arrive, device):
        return pltpu.make_async_remote_copy(
            src_ref=source, dst_ref=target, send_sem=send, recv_sem=arrive, device_id=device, device_id_type=MESH
        )

    def slot_rows(k):
        return pl.ds(EDGE * k, EDGE)

    direct_copies = [
        [
            remote(
                sent.at[turn, slot_rows(k)], recv.at[turn, j], edge_send.at[turn, j], edge_recv.at[turn, j],
                (shifted(offset), shard),
            )
            for j, (k, offset) in enumerate(((1, -1), (0, 1), (4, regions // 2)))
        ]
        for turn in range(ITERS)
    ]
    hold = (hold_a, hold_b)

    def out_copy(turn, r):
        return remote(tiles.at[turn, r], hold[turn].at[region], hop_send.at[turn, 0], hop_recv.at[turn, 0], (r, shard))

    def on_copy(turn, r):
        return remote(moved.at[turn, r], reached.at[turn, region], hop_send.at[turn, 1], hop_recv.at[turn, 1], (r, shard))

    def all_tiles(turn, step):
        ref = (hold[turn] if step == 0 else reached.at[turn]).at[pl.ds(0, regions - 1)]
        return remote(ref, ref, hop_send.at[turn, step], hop_recv.at[turn, step], (shifted(1), shard))

    part_copies = [
        [
            remote(part.at[turn], gathered.at[turn, j], part_send.at[turn, j], part_recv.at[turn, j], (region, peers[j]))
            for j in range(shards - 1)
        ]
        for turn in range(ITERS)
    ]

    def backward():
        stride = lax.rem(neighbours[2, 0] + regions, regions)
        return jnp.where(region < regions // 2, regions - stride, stride)

    def alive(n):
        return jnp.where((shard * blocks + n) * BLK < points[region], f32(1.0), f32(0.0))

    def rows_of(n):
        return pl.ds(pl.multiple_of(n * BLK, BLK), BLK)

    def each(body, init=0):
        return lax.fori_loop(0, blocks, body, init, unroll=unroll)

    def post_edges(turn, n, edges):
        sent[turn, :, rows_of(n)] = edges
        for group in range(regions // blocks):
            start = 2 * EDGE + TILE * group
            tiles[turn, group * blocks + n] = edges[start : start + TILE]

    def send_edges(turn):
        hold[turn][region] = tiles[turn, region]
        others(lambda r: out_copy(turn, r).start())
        for copy in direct_copies[turn]:
            copy.start()

    def send_part(turn, total_part):
        for i in range(MOMENTS):
            part[turn, i] = total_part[i : i + 1, :]
        for copy in part_copies[turn]:
            copy.start()

    with jax.named_scope("onehot"):
        loads[5].wait()
        onehot_f[...] = jnp.zeros_like(onehot_f)
        lane = lax.broadcasted_iota(jnp.int32, (1, cell_count), 1)
        for k in range(NBR):
            for i in range(EDGE):
                row = EDGE * k + i
                onehot_f[row : row + 1, :] = (lane == cells[k, 0, i]).astype(f32)
        picks = onehot_f[...]
        onehot[...] = picks.astype(bf16)
        half = (inflow_step * picks[0:width]).astype(bf16)
        halved[3 * width :, :] = jnp.zeros((WIDE - 3 * width, cell_count), bf16)
        for i in range(3):
            halved[i * width : (i + 1) * width, :] = half

    with jax.named_scope("wait_dist"):
        loads[6].wait()
        loads[0].wait()
        loads[3].start()
        loads[4].start()

    def first_edges(n, carry):
        high, low = halves(dist[rows_of(n), :] * alive(n))
        pick = onehot[0:width]
        post_edges(0, n, across(pick, high) + across(pick, low))
        return carry

    with jax.named_scope("first_edges"):
        each(first_edges)

    with jax.named_scope("entry"):
        pl.semaphore_wait(barrier, regions + shards - 2)
        send_edges(0)

    with jax.named_scope("basis"):
        loads[1].wait()
        loads[2].wait()
        loads[7].wait()
        total = points[region]
        x, y, z = vel[0], vel[1], vel[2]
        place = shard * local + lax.broadcasted_iota(jnp.int32, (1, local), 1)
        scale = f32(VMAX) / jnp.full((1, local), total.astype(f32))
        quad = weights[...] * scale * (place < total).astype(f32)
        basis_f[...] = jnp.zeros_like(basis_f)
        for i, row in enumerate(moment_rows(x, y, z)):
            basis_f[i : i + 1, :] = row * quad

        def split_basis(n, carry):
            high, low = halves(basis_f[:, rows_of(n)])
            basis[n, 0:BASIS, 0:BLK] = high
            basis[n, 0:BASIS, BLK : 2 * BLK] = high
            basis[n, BASIS : 2 * BASIS, 0:BLK] = low
            basis[n, BASIS : 2 * BASIS, BLK : 2 * BLK] = jnp.zeros_like(low)
            return carry

        each(split_basis)

    def weighted(n, high, low):
        both = plain(basis[n], jnp.concatenate([high, low], axis=0))
        return both[:BASIS] + both[BASIS:]

    def first_moments(n, acc):
        high, low = halves(dist[rows_of(n), :] * alive(n))
        return acc + weighted(n, high, low)

    with jax.named_scope("first_moments"):
        send_part(0, each(first_moments, jnp.zeros((BASIS, cell_count), f32)))

    with jax.named_scope("turn_columns"):
        basis_f[0:3, :] = jnp.concatenate([x, y, z], axis=0)

        def turn_columns(n, carry):
            turned = jnp.transpose(basis_f[0:8, rows_of(n)])
            for axis in range(3):
                columns[axis, rows_of(n), :] = jnp.broadcast_to(turned[:, axis : axis + 1], (BLK, 128))
            return carry

        each(turn_columns)
        pieces[...] = jnp.zeros_like(pieces)
        flow_t[...] = jnp.zeros_like(flow_t)

    def forward(turn):
        all_tiles(turn, 0).wait_recv()

        back = backward()

        def take(r, carry):
            moved[turn, r] = hold[turn][lax.rem(r + back, regions)]
            return carry

        lax.fori_loop(0, regions, take, 0, unroll=8)
        reached[turn, region] = moved[turn, region]
        others(lambda r: on_copy(turn, r).start())

    def prepare_inv(n, carry):
        high, low = halves(inv[n])
        both_inv[n, :, 0:cell_count] = high
        both_inv[n, :, cell_count : 2 * cell_count] = low
        edges = plain(onehot[0:width], jnp.concatenate([high, low], axis=1)).astype(bf16)
        both_edge[n, 0:width, 0:cell_count] = edges[:, 0:cell_count]
        both_edge[n, 0:width, cell_count : 2 * cell_count] = edges[:, 0:cell_count]
        both_edge[n, width : 2 * width, 0:cell_count] = edges[:, cell_count : 2 * cell_count]
        both_edge[n, width : 2 * width, cell_count : 2 * cell_count] = jnp.zeros((width, cell_count), bf16)
        back_h = across(halved[0:width], high).astype(bf16)
        inv_edge[n, 0:width] = back_h
        inv_edge[n, width : 2 * width] = back_h
        inv_edge[n, 2 * width : WIDE] = across(halved[2 * width : WIDE], low).astype(bf16)
        near = across(edges[:, 0:cell_count], halved[...])
        fine = across(edges[:, cell_count : 2 * cell_count], halved[...])
        lane = lax.broadcasted_iota(jnp.int32, (width, WIDE), 1)
        edge_edge[n] = jnp.where(lane < 2 * width, near, fine).astype(bf16)
        return carry

    def prepare_mat(n, carry):
        for k in range(NBR):
            high, low = halves(interp[k, rows_of(n), :])
            mats[n, k, :, 0:BLK] = high
            mats[n, k, :, BLK : 2 * BLK] = low
        return carry

    with jax.named_scope("prepare_inv"):
        loads[3].wait()
        each(prepare_inv)
    with jax.named_scope("prepare_mat"):
        loads[4].wait()
        each(prepare_mat)
    with jax.named_scope("forward0"):
        forward(0)

    def collect(turn):
        for copy in part_copies[turn]:
            copy.wait_recv()
        moments = part[turn]
        for j in range(shards - 1):
            moments = moments + gathered[turn, j]
        rows = cell_rows([moments[i] for i in range(MOMENTS)])
        for i, row in enumerate(rows):
            coef[i : i + 1, :] = row

    def relax(n, carry):
        on = alive(n)
        chunk = 32
        for tile in range(cell_count // 128):
            lanes = pl.ds(128 * tile, 128)
            front, u, v, w, fall, skew_x, skew_y, skew_z = [coef[i : i + 1, lanes] for i in range(8)]
            for c in range(BLK // chunk):
                rows = pl.ds(pl.multiple_of(n * BLK + c * chunk, chunk), chunk)
                e_x = columns[0, rows, :] - u
                e_y = columns[1, rows, :] - v
                e_z = columns[2, rows, :] - w
                power = (e_x * e_x + e_y * e_y + e_z * e_z) * fall
                lean = e_x * skew_x + e_y * skew_y + e_z * skew_z
                value = front * jnp.exp(power) * (1.0 + lean * (power + 2.5))
                rhs[rows, lanes] = dist[rows, lanes] * on + value
        return carry

    def place_in(k, value):
        high, low = halves(value)
        for n in range(blocks):
            lanes = slice(BLK * n, BLK * (n + 1))
            pieces[n, k, 0:EDGE, 0:BLK] = high[:, lanes]
            pieces[n, k, 0:EDGE, BLK : 2 * BLK] = high[:, lanes]
            pieces[n, k, EDGE : 2 * EDGE, 0:BLK] = low[:, lanes]

    def interpolate(interfaces, done):
        def one(n, carry):
            for k in interfaces:
                both = across(pieces[n, k], mats[n, k])
                high, low = halves(both[:EDGE] + both[EDGE:])
                flow_t[n, EDGE * k : EDGE * (k + 1)] = high
                flow_t[n, width + EDGE * k : width + EDGE * (k + 1)] = low
                flow_t[n, 2 * width + EDGE * k : 2 * width + EDGE * (k + 1)] = high
            if done:
                flow[n] = jnp.transpose(flow_t[n])
            return carry

        each(one)

    def arrive_direct(turn):
        for j, k in enumerate((0, 1, 4)):
            direct_copies[turn][j].wait_recv()
            place_in(k, recv[turn, j])
        interpolate((0, 1, 4), False)

    def arrive(turn):
        all_tiles(turn, 1).wait_recv()
        for k, first in ((3, 0), (2, 2 * blocks)):
            rows = [[reached[turn, first + g * blocks + n] for n in range(blocks)] for g in range(2)]
            place_in(k, jnp.concatenate([jnp.concatenate(r, axis=1) for r in rows], axis=0))

    with jax.named_scope("direct0"):
        arrive_direct(0)
    with jax.named_scope("collect0"):
        collect(0)
    with jax.named_scope("relax0"):
        each(relax)

    def main_edges(n, carry):
        high, low = halves(rhs[rows_of(n), :])
        edges = across(both_edge[n], jnp.concatenate([high, low], axis=1))
        kept[n] = edges[:width] + edges[width:]
        return carry

    def main_moments(n, acc):
        high, low = halves(rhs[rows_of(n), :])
        held_h, held_l = halves(weighted(n, high, low))
        held = jnp.concatenate(
            [
                jnp.concatenate([held_h, held_h], axis=1),
                jnp.concatenate([held_l, jnp.zeros_like(held_l)], axis=1),
            ],
            axis=0,
        )
        both = across(held, both_inv[n])
        return acc + both[:BASIS] + both[BASIS:]

    with jax.named_scope("main_edges"):
        each(main_edges)
    with jax.named_scope("main_moments"):
        main_part = each(main_moments, jnp.zeros((BASIS, cell_count), f32))
    with jax.named_scope("arrive0"):
        arrive(0)
    with jax.named_scope("interpolate0"):
        interpolate((2, 3), True)

    def landed_edges(n, carry):
        post_edges(1, n, (kept[n] + plain(edge_edge[n], flow_t[n])) * alive(n))
        return carry

    def landed_moments(n, acc):
        both = plain(basis[n, :, 0:BLK], flow[n])
        held_h, held_l = halves(both[:BASIS] + both[BASIS:])
        both = plain(jnp.concatenate([held_h, held_l], axis=0), inv_edge[n])
        return acc + both[:BASIS] + both[BASIS:]

    with jax.named_scope("landed_edges"):
        each(landed_edges)
        send_edges(1)
    with jax.named_scope("landed_moments"):
        send_part(1, each(landed_moments, main_part))
    with jax.named_scope("forward1"):
        forward(1)
    with jax.named_scope("direct1"):
        arrive_direct(1)
    with jax.named_scope("collect1"):
        collect(1)
    with jax.named_scope("relax1"):
        each(relax)

    def main_result(n, carry):
        high, low = halves(rhs[rows_of(n), :])
        wide = jnp.concatenate(
            [
                jnp.concatenate([high, high], axis=1),
                jnp.concatenate([low, jnp.zeros_like(low)], axis=1),
            ],
            axis=0,
        )
        turned = across(both_inv[n], wide)
        out[0, rows_of(n), :] = jnp.transpose(turned[:, :BLK] + turned[:, BLK:])
        return carry

    def last(n, carry):
        out[0, rows_of(n), :] = (out[0, rows_of(n), :] + plain(flow[n], inv_edge[n])) * alive(n)
        return carry

    with jax.named_scope("main_result"):
        each(main_result)
    with jax.named_scope("arrive1"):
        arrive(1)
    with jax.named_scope("interpolate1"):
        interpolate((2, 3), True)
    with jax.named_scope("last"):
        each(last)
    with jax.named_scope("finish"):
        for turn in range(ITERS):
            for copy in part_copies[turn] + direct_copies[turn]:
                copy.wait_send()
            for step in range(2):
                all_tiles(turn, step).wait_send()


def update(regions, shards, unroll, *arrays):
    distribution, velocity, weights, points, neighbours, cells, interpolation, inverse = arrays
    local, cell_count = distribution.shape[1:]
    blocks = local // BLK
    width = NBR * EDGE
    anywhere = pl.BlockSpec(memory_space=pl.ANY)
    vmem = pltpu.VMEM
    signals = pltpu.SemaphoreType.DMA
    return pl.pallas_call(
        functools.partial(kernel, regions, shards, unroll),
        out_shape=jax.ShapeDtypeStruct((1, local, cell_count), f32),
        in_specs=[anywhere] * 8,
        out_specs=pl.BlockSpec(memory_space=pltpu.VMEM),
        scratch_shapes=[
            pltpu.SMEM(points.shape, jnp.int32),
            pltpu.SMEM(neighbours.shape, jnp.int32),
            pltpu.SMEM(cells.shape, jnp.int32),
            vmem((local, cell_count), f32),
            vmem((3, 1, local), f32),
            vmem((1, local), f32),
            vmem((NBR, local, BLK), f32),
            vmem((blocks, cell_count, cell_count), f32),
            vmem((blocks, cell_count, 2 * cell_count), bf16),
            vmem((blocks, 2 * width, 2 * cell_count), bf16),
            vmem((blocks, width, WIDE), bf16),
            vmem((blocks, WIDE, cell_count), bf16),
            vmem((blocks, NBR, BLK, 2 * BLK), bf16),
            vmem((BASIS, local), f32),
            vmem((blocks, 2 * BASIS, 2 * BLK), bf16),
            vmem((3, local, 128), f32),
            vmem((PAD, cell_count), f32),
            vmem((PAD, cell_count), bf16),
            vmem((WIDE, cell_count), bf16),
            vmem((blocks, NBR, 2 * EDGE, 2 * BLK), bf16),
            vmem((blocks, WIDE, BLK), bf16),
            vmem((blocks, BLK, WIDE), bf16),
            vmem((blocks, width, BLK), f32),
            vmem((ITERS, width, local), f32),
            vmem((ITERS, 3, EDGE, local), f32),
            vmem((ITERS, regions, TILE, BLK), f32),
            vmem((regions, TILE, BLK), f32),
            vmem((regions, TILE, BLK), f32),
            vmem((ITERS, regions, TILE, BLK), f32),
            vmem((ITERS, regions, TILE, BLK), f32),
            vmem((ITERS, MOMENTS, 1, cell_count), f32),
            vmem((ITERS, shards - 1, MOMENTS, 1, cell_count), f32),
            vmem((8, cell_count), f32),
            vmem((local, cell_count), f32),
            signals((8,)),
            signals((ITERS, 3)),
            signals((ITERS, 3)),
            signals((ITERS, 2)),
            signals((ITERS, 2)),
            signals((ITERS, shards - 1)),
            signals((ITERS, shards - 1)),
        ],
        compiler_params=pltpu.CompilerParams(
            collective_id=0, has_side_effects=True, vmem_limit_bytes=56 * 1024 * 1024
        ),
    )(distribution, velocity, weights, points, neighbours, cells, interpolation, inverse)


def solution(mesh):
    regions, shards = mesh.shape["region"], mesh.shape["vel"]

    def local(distribution, velocity, weights, grid_points, neighbours, interface_cells, interpolation, block_inverse):
        return update(
            regions, shards, 8,
            distribution, velocity.transpose(1, 0, 2), weights, grid_points, neighbours.T,
            interface_cells.transpose(1, 0, 2), interpolation, block_inverse,
        )

    placed = (
        P("region", "vel", None),
        P("region", None, "vel"),
        P("region", "vel"),
        P(),
        P(),
        P("region", None, None),
        P("region", None, "vel", None),
        P("region", "vel", None, None),
    )
    return jax.shard_map(
        local, mesh=mesh, in_specs=placed, out_specs=P("region", "vel", None), check_vma=False
    )
```

```python
import functools
import math

import jax
import jax.numpy as jnp
from jax import lax
from jax.experimental import pallas as pl
from jax.experimental.pallas import tpu as pltpu
from jax.sharding import PartitionSpec as P

VMAX = 8192
BLK = 128
EDGE = 16
NBR = 5
ITERS = 2
PAD = 128
WIDE = 256
BASIS = 16
MOMENTS = 13
TILE = 8

relax_step = 0.5
inflow_step = 0.5
viscous_conductive_ratio = 2.0 / 3.0

MESH = pl.DeviceIdType.MESH
f32 = jnp.float32
bf16 = jnp.bfloat16


def far_first(regions):
    side = math.isqrt(regions // 2)

    def hops(offset):
        total = 0
        for region in range(regions):
            here, there = region // 2, (region + offset) % regions // 2
            for a, b in ((here // side, there // side), (here % side, there % side)):
                total += min((a - b) % side, (b - a) % side)
        return total

    return sorted(range(1, regions), key=lambda offset: (-hops(offset), offset))


def across(a, b):
    return lax.dot_general(a, b, (((1,), (1,)), ((), ())), preferred_element_type=f32)


def plain(a, b):
    return jnp.dot(a, b, preferred_element_type=f32)


def halves(x):
    high = x.astype(bf16)
    return high, (x - high.astype(f32)).astype(bf16)


def moment_rows(x, y, z):
    speed_sq = x * x + y * y + z * z
    return [
        jnp.ones_like(x), x, y, z,
        x * x, y * y, z * z,
        x * y, x * z, y * z,
        x * speed_sq, y * speed_sq, z * speed_sq,
    ]


def cell_rows(m):
    density = m[0]
    over = 1.0 / density
    u, v, w = m[1] * over, m[2] * over, m[3] * over
    energy = m[4] + m[5] + m[6]
    flow_sq = u * u + v * v + w * w
    warmth = (energy * over - flow_sq) / 3.0
    stress_x = m[4] * u + m[7] * v + m[8] * w
    stress_y = m[7] * u + m[5] * v + m[9] * w
    stress_z = m[8] * u + m[9] * v + m[6] * w
    drift = 2.0 * density * flow_sq
    heat_x = 0.5 * (m[10] - 2.0 * stress_x - u * energy + drift * u)
    heat_y = 0.5 * (m[11] - 2.0 * stress_y - v * energy + drift * v)
    heat_z = 0.5 * (m[12] - 2.0 * stress_z - w * energy + drift * w)
    hot = 2.0 * math.pi * warmth
    front = relax_step * density / (hot * jnp.sqrt(hot))
    fall = -0.5 / warmth
    skew = (-2.0 * (1.0 - viscous_conductive_ratio)) / (5.0 * density * warmth * warmth)
    return [front, u, v, w, fall, heat_x * skew, heat_y * skew, heat_z * skew]


def kernel(
    regions, shards, unroll,
    dist_hbm, vel_hbm, weights_hbm, points_hbm, neighbours_hbm, cells_hbm, interp_hbm, inv_hbm, out_hbm,
    points, neighbours, cells, dist, vel, weights, interp, inv, both_inv, both_edge, edge_edge, inv_edge, mats,
    basis_f, basis, columns, onehot_f, onehot, halved, spread, pieces, flow_t, flow, kept, sent, recv, tiles, hold_a, hold_b, moved, reached, part, gathered, coef, rhs, held, falls, out,
    in_sem, out_sem, edge_send, edge_recv, hop_send, hop_recv, part_send, part_recv,
):
    region = lax.axis_index("region")
    shard = lax.axis_index("vel")
    local, cell_count = dist.shape
    blocks = local // BLK
    width = NBR * EDGE

    def shifted(offset):
        return lax.rem(region + offset + regions, regions)

    steps = sorted(range(1, shards), key=lambda step: -min(step, shards - step))
    peers = [lax.rem(shard + step, shards) for step in steps]
    offsets = far_first(regions)
    barrier = pltpu.get_barrier_semaphore()

    def others(body):
        for offset in offsets:
            body(shifted(offset))

    for peer in peers:
        pl.semaphore_signal(barrier, inc=1, device_id=(region, peer), device_id_type=MESH)
    others(lambda r: pl.semaphore_signal(barrier, inc=1, device_id=(r, shard), device_id_type=MESH))

    loads = [
        pltpu.make_async_copy(source, target, in_sem.at[i])
        for i, (source, target) in enumerate(
            [
                (dist_hbm.at[0], dist),
                (vel_hbm, vel),
                (weights_hbm, weights),
                (inv_hbm.at[0], inv),
                (interp_hbm.at[0], interp),
                (cells_hbm, cells),
                (points_hbm, points),
                (neighbours_hbm, neighbours),
            ]
        )
    ]
    for i in (5, 6, 0, 7, 1, 2):
        loads[i].start()

    def remote(source, target, send, arrive, device):
        return pltpu.make_async_remote_copy(
            src_ref=source, dst_ref=target, send_sem=send, recv_sem=arrive, device_id=device, device_id_type=MESH
        )

    def slot_rows(k):
        return pl.ds(EDGE * k, EDGE)

    direct_copies = [
        [
            remote(
                sent.at[turn, slot_rows(k)], recv.at[turn, j], edge_send.at[turn, j], edge_recv.at[turn, j],
                (shifted(offset), shard),
            )
            for j, (k, offset) in enumerate(((1, -1), (0, 1), (4, regions // 2)))
        ]
        for turn in range(ITERS)
    ]
    hold = (hold_a, hold_b)

    def out_copy(turn, r):
        return remote(tiles.at[turn, r], hold[turn].at[region], hop_send.at[turn, 0], hop_recv.at[turn, 0], (r, shard))

    def on_copy(turn, r):
        return remote(moved.at[turn, r], reached.at[turn, region], hop_send.at[turn, 1], hop_recv.at[turn, 1], (r, shard))

    def all_tiles(turn, step):
        ref = (hold[turn] if step == 0 else reached.at[turn]).at[pl.ds(0, regions - 1)]
        return remote(ref, ref, hop_send.at[turn, step], hop_recv.at[turn, step], (shifted(1), shard))

    part_copies = [
        [
            remote(part.at[turn], gathered.at[turn, j], part_send.at[turn, j], part_recv.at[turn, j], (region, peers[j]))
            for j in range(shards - 1)
        ]
        for turn in range(ITERS)
    ]

    def backward():
        stride = lax.rem(neighbours[2, 0] + regions, regions)
        return jnp.where(region < regions // 2, regions - stride, stride)

    def alive(n):
        return jnp.where((shard * blocks + n) * BLK < points[region], f32(1.0), f32(0.0))

    def rows_of(n):
        return pl.ds(pl.multiple_of(n * BLK, BLK), BLK)

    def each(body, init=0):
        return lax.fori_loop(0, blocks, body, init, unroll=unroll)

    def post_edges(turn, n, edges):
        sent[turn, :, rows_of(n)] = edges
        for group in range(regions // blocks):
            start = 2 * EDGE + TILE * group
            tiles[turn, group * blocks + n] = edges[start : start + TILE]

    def send_edges(turn):
        hold[turn][region] = tiles[turn, region]
        others(lambda r: out_copy(turn, r).start())
        for copy in direct_copies[turn]:
            copy.start()

    def send_part(turn, total_part):
        for i in range(MOMENTS):
            part[turn, i] = total_part[i : i + 1, :]
        for copy in part_copies[turn]:
            copy.start()

    with jax.named_scope("onehot"):
        loads[5].wait()
        onehot_f[...] = jnp.zeros_like(onehot_f)
        lane = lax.broadcasted_iota(jnp.int32, (1, cell_count), 1)
        for k in range(NBR):
            for i in range(EDGE):
                row = EDGE * k + i
                onehot_f[row : row + 1, :] = (lane == cells[k, 0, i]).astype(f32)
        picks = onehot_f[...]
        onehot[...] = picks.astype(bf16)
        half = (inflow_step * picks[0:width]).astype(bf16)
        halved[3 * width :, :] = jnp.zeros((WIDE - 3 * width, cell_count), bf16)
        spread[2 * width :, :] = jnp.zeros((WIDE - 2 * width, cell_count), bf16)
        for i in range(2):
            spread[i * width : (i + 1) * width, :] = half
        for i in range(3):
            halved[i * width : (i + 1) * width, :] = half

    with jax.named_scope("wait_dist"):
        loads[6].wait()
        loads[0].wait()
        loads[3].start()
        loads[4].start()

    def first_edges(n, carry):
        high, low = halves(dist[rows_of(n), :] * alive(n))
        pick = onehot[0:width]
        twice = jnp.concatenate([pick, pick], axis=1)
        post_edges(0, n, across(twice, jnp.concatenate([high, low], axis=1)))
        return carry

    with jax.named_scope("first_edges"):
        each(first_edges)

    with jax.named_scope("entry"):
        pl.semaphore_wait(barrier, regions + shards - 2)
        send_edges(0)

    with jax.named_scope("basis"):
        loads[1].wait()
        loads[2].wait()
        loads[7].wait()
        total = points[region]
        x, y, z = vel[0], vel[1], vel[2]
        place = shard * local + lax.broadcasted_iota(jnp.int32, (1, local), 1)
        scale = f32(VMAX) / jnp.full((1, local), total.astype(f32))
        quad = weights[...] * scale * (place < total).astype(f32)
        basis_f[...] = jnp.zeros_like(basis_f)
        for i, row in enumerate(moment_rows(x, y, z)):
            basis_f[i : i + 1, :] = row * quad

        def split_basis(n, carry):
            high, low = halves(basis_f[:, rows_of(n)])
            basis[n, 0:BASIS, 0:BLK] = high
            basis[n, 0:BASIS, BLK : 2 * BLK] = high
            basis[n, BASIS : 2 * BASIS, 0:BLK] = low
            basis[n, BASIS : 2 * BASIS, BLK : 2 * BLK] = jnp.zeros_like(low)
            return carry

        each(split_basis)

    def weighted(n, high, low):
        both = plain(basis[n], jnp.concatenate([high, low], axis=0))
        return both[:BASIS] + both[BASIS:]

    def first_moments(n, acc):
        high, low = halves(dist[rows_of(n), :] * alive(n))
        return acc + weighted(n, high, low)

    with jax.named_scope("first_moments"):
        send_part(0, each(first_moments, jnp.zeros((BASIS, cell_count), f32)))

    with jax.named_scope("turn_columns"):
        basis_f[0:3, :] = jnp.concatenate([x, y, z], axis=0)

        def turn_columns(n, carry):
            turned = jnp.transpose(basis_f[0:8, rows_of(n)])
            for axis in range(3):
                columns[axis, rows_of(n), :] = jnp.broadcast_to(turned[:, axis : axis + 1], (BLK, 128))
            return carry

        each(turn_columns)
        pieces[...] = jnp.zeros_like(pieces)
        flow_t[...] = jnp.zeros_like(flow_t)

    def forward(turn):
        all_tiles(turn, 0).wait_recv()

        back = backward()

        def take(r, carry):
            moved[turn, r] = hold[turn][lax.rem(r + back, regions)]
            return carry

        lax.fori_loop(0, regions, take, 0, unroll=8)
        reached[turn, region] = moved[turn, region]
        others(lambda r: on_copy(turn, r).start())

    def prepare_inv(n, carry):
        high, low = halves(inv[n])
        both_inv[n, :, 0:cell_count] = high
        both_inv[n, :, cell_count : 2 * cell_count] = low
        edges = plain(onehot[0:width], jnp.concatenate([high, low], axis=1)).astype(bf16)
        both_edge[n, 0:width, 0:cell_count] = edges[:, 0:cell_count]
        both_edge[n, 0:width, cell_count : 2 * cell_count] = edges[:, 0:cell_count]
        both_edge[n, width : 2 * width, 0:cell_count] = edges[:, cell_count : 2 * cell_count]
        both_edge[n, width : 2 * width, cell_count : 2 * cell_count] = jnp.zeros((width, cell_count), bf16)
        return carry

    def prepare_edge_edge(group, carry):
        rows = both_edge[pl.ds(2 * group, 2), :, 0:cell_count].reshape(4 * width, cell_count)
        value = across(rows, halved[...])
        lane = lax.broadcasted_iota(jnp.int32, (width, WIDE), 1)
        for i in range(2):
            near = value[2 * i * width : (2 * i + 1) * width]
            fine = value[(2 * i + 1) * width : (2 * i + 2) * width]
            edge_edge[2 * group + i] = jnp.where(lane < 2 * width, near, fine).astype(bf16)
        return carry

    def prepare_inv_edge(n, carry):
        back_h = across(halved[0:width], both_inv[n, :, 0:cell_count]).astype(bf16)
        inv_edge[n, 0:width] = back_h
        inv_edge[n, width : 2 * width] = back_h
        inv_edge[n, 2 * width : WIDE] = across(
            halved[2 * width : WIDE], both_inv[n, :, cell_count : 2 * cell_count]
        ).astype(bf16)
        return carry

    def prepare_mat(n, carry):
        for k in range(NBR):
            high, low = halves(interp[k, rows_of(n), :])
            mats[n, k, :, 0:BLK] = high
            mats[n, k, :, BLK : 2 * BLK] = low
        return carry

    with jax.named_scope("prepare_inv"):
        loads[3].wait()
        each(prepare_inv)
        lax.fori_loop(0, blocks // 2, prepare_edge_edge, 0, unroll=unroll)
    with jax.named_scope("forward0"):
        forward(0)
    with jax.named_scope("prepare_mat"):
        loads[4].wait()
        each(prepare_mat)

    def collect(turn):
        for copy in part_copies[turn]:
            copy.wait_recv()
        moments = part[turn]
        for j in range(shards - 1):
            moments = moments + gathered[turn, j]
        rows = cell_rows([moments[i] for i in range(MOMENTS)])
        for i, row in enumerate(rows):
            coef[i : i + 1, :] = row

    def relax(n, carry):
        on = alive(n)
        chunk = 32
        for tile in range(cell_count // 128):
            lanes = pl.ds(128 * tile, 128)
            front, u, v, w, fall, skew_x, skew_y, skew_z = [coef[i : i + 1, lanes] for i in range(8)]
            for c in range(BLK // chunk):
                rows = pl.ds(pl.multiple_of(n * BLK + c * chunk, chunk), chunk)
                e_x = columns[0, rows, :] - u
                e_y = columns[1, rows, :] - v
                e_z = columns[2, rows, :] - w
                power = (e_x * e_x + e_y * e_y + e_z * e_z) * fall
                lean = e_x * skew_x + e_y * skew_y + e_z * skew_z
                value = front * jnp.exp(power) * (1.0 + lean * (power + 2.5))
                rhs[rows, lanes] = dist[rows, lanes] * on + value
        return carry

    def place_in(k, value):
        high, low = halves(value)
        for n in range(blocks):
            lanes = slice(BLK * n, BLK * (n + 1))
            pieces[n, k, 0:EDGE, 0:BLK] = high[:, lanes]
            pieces[n, k, 0:EDGE, BLK : 2 * BLK] = high[:, lanes]
            pieces[n, k, EDGE : 2 * EDGE, 0:BLK] = low[:, lanes]

    def interpolate(interfaces, done):
        def one(n, carry):
            for k in interfaces:
                both = across(pieces[n, k], mats[n, k])
                high, low = halves(both[:EDGE] + both[EDGE:])
                flow_t[n, EDGE * k : EDGE * (k + 1)] = high
                flow_t[n, width + EDGE * k : width + EDGE * (k + 1)] = low
                flow_t[n, 2 * width + EDGE * k : 2 * width + EDGE * (k + 1)] = high
            if done:
                flow[n] = jnp.transpose(flow_t[n])
            return carry

        each(one)

    def arrive_direct(turn):
        for j, k in enumerate((0, 1, 4)):
            direct_copies[turn][j].wait_recv()
            place_in(k, recv[turn, j])
        interpolate((0, 1, 4), False)

    def arrive(turn):
        all_tiles(turn, 1).wait_recv()
        for k, first in ((3, 0), (2, 2 * blocks)):
            rows = [[reached[turn, first + g * blocks + n] for n in range(blocks)] for g in range(2)]
            place_in(k, jnp.concatenate([jnp.concatenate(r, axis=1) for r in rows], axis=0))

    with jax.named_scope("direct0"):
        arrive_direct(0)
    with jax.named_scope("collect0"):
        collect(0)
    with jax.named_scope("relax0"):
        each(relax)

    def main_edges(n, carry):
        high, low = halves(rhs[rows_of(n), :])
        edges = across(both_edge[n], jnp.concatenate([high, low], axis=1))
        kept[n] = edges[:width] + edges[width:]
        return carry

    def main_moments(n, carry):
        high, low = halves(rhs[rows_of(n), :])
        held[n] = weighted(n, high, low)
        return carry

    with jax.named_scope("main_edges"):
        each(main_edges)
    with jax.named_scope("main_moments"):
        each(main_moments)
    with jax.named_scope("inv_edge0"):
        lax.fori_loop(0, blocks // 2, prepare_inv_edge, 0, unroll=unroll)
    with jax.named_scope("arrive0"):
        arrive(0)
    with jax.named_scope("interpolate0"):
        interpolate((2, 3), True)

    def landed_edges(n, carry):
        post_edges(1, n, (kept[n] + plain(edge_edge[n], flow_t[n])) * alive(n))
        return carry

    def fall_moments(n, carry):
        both = plain(basis[n, :, 0:BLK], flow[n])
        fall_h, fall_l = halves(both[:BASIS] + both[BASIS:])
        falls[n, 0:BASIS] = fall_h
        falls[n, BASIS : 2 * BASIS] = fall_l
        return carry

    def landed_moments():
        each(fall_moments)
        spreads = plain(falls[...].reshape(2 * BASIS * blocks, WIDE), spread[...])
        acc = jnp.zeros((BASIS, cell_count), f32)
        for n in range(blocks):
            start = 2 * BASIS * n
            both = spreads[start : start + BASIS] + spreads[start + BASIS : start + 2 * BASIS]
            held_h, held_l = halves(held[n] + both)
            both = across(
                jnp.concatenate(
                    [
                        jnp.concatenate([held_h, held_h], axis=1),
                        jnp.concatenate([held_l, jnp.zeros_like(held_l)], axis=1),
                    ],
                    axis=0,
                ),
                both_inv[n],
            )
            acc = acc + both[:BASIS] + both[BASIS:]
        return acc

    with jax.named_scope("landed_edges"):
        each(landed_edges)
        send_edges(1)
    with jax.named_scope("landed_moments"):
        send_part(1, landed_moments())
    with jax.named_scope("inv_edge1"):
        lax.fori_loop(blocks // 2, blocks, prepare_inv_edge, 0, unroll=unroll)
    with jax.named_scope("forward1"):
        forward(1)
    with jax.named_scope("direct1"):
        arrive_direct(1)
    with jax.named_scope("collect1"):
        collect(1)
    with jax.named_scope("relax1"):
        each(relax)

    def main_result(n, carry):
        high, low = halves(rhs[rows_of(n), :])
        wide = jnp.concatenate(
            [
                jnp.concatenate([high, high], axis=1),
                jnp.concatenate([low, jnp.zeros_like(low)], axis=1),
            ],
            axis=0,
        )
        turned = across(both_inv[n], wide)
        out[rows_of(n), :] = jnp.transpose(turned[:, :BLK] + turned[:, BLK:])
        return carry

    def last(n, carry):
        out[rows_of(n), :] = (out[rows_of(n), :] + plain(flow[n], inv_edge[n])) * alive(n)
        pltpu.make_async_copy(out.at[rows_of(n)], out_hbm.at[0, rows_of(n)], out_sem.at[n]).start()
        return carry

    with jax.named_scope("main_result"):
        each(main_result)
    with jax.named_scope("arrive1"):
        arrive(1)
    with jax.named_scope("interpolate1"):
        interpolate((2, 3), True)
    with jax.named_scope("last"):
        each(last)
    with jax.named_scope("finish"):
        for n in range(blocks):
            pltpu.make_async_copy(out.at[rows_of(n)], out_hbm.at[0, rows_of(n)], out_sem.at[n]).wait()
        for turn in range(ITERS):
            for copy in part_copies[turn] + direct_copies[turn]:
                copy.wait_send()
            for step in range(2):
                all_tiles(turn, step).wait_send()


def hand_on(value_hbm, out_hbm, held, in_sems, out_sems):
    parts = in_sems.shape[0]
    rows = held.shape[0] // parts
    ways = [pl.ds(i * rows, rows) for i in range(parts)]
    takes = [pltpu.make_async_copy(value_hbm.at[0, way], held.at[way], in_sems.at[i]) for i, way in enumerate(ways)]
    gives = [pltpu.make_async_copy(held.at[way], out_hbm.at[0, way], out_sems.at[i]) for i, way in enumerate(ways)]
    for take in takes:
        take.start()
    for take, give in zip(takes, gives):
        take.wait()
        give.start()
    for give in gives:
        give.wait()


def update(regions, shards, unroll, *arrays):
    distribution, velocity, weights, points, neighbours, cells, interpolation, inverse = arrays
    local, cell_count = distribution.shape[1:]
    blocks = local // BLK
    width = NBR * EDGE
    anywhere = pl.BlockSpec(memory_space=pl.ANY)
    vmem = pltpu.VMEM
    signals = pltpu.SemaphoreType.DMA
    value = pl.pallas_call(
        functools.partial(kernel, regions, shards, unroll),
        out_shape=jax.ShapeDtypeStruct((1, local, cell_count), f32),
        in_specs=[anywhere] * 8,
        out_specs=anywhere,
        scratch_shapes=[
            pltpu.SMEM(points.shape, jnp.int32),
            pltpu.SMEM(neighbours.shape, jnp.int32),
            pltpu.SMEM(cells.shape, jnp.int32),
            vmem((local, cell_count), f32),
            vmem((3, 1, local), f32),
            vmem((1, local), f32),
            vmem((NBR, local, BLK), f32),
            vmem((blocks, cell_count, cell_count), f32),
            vmem((blocks, cell_count, 2 * cell_count), bf16),
            vmem((blocks, 2 * width, 2 * cell_count), bf16),
            vmem((blocks, width, WIDE), bf16),
            vmem((blocks, WIDE, cell_count), bf16),
            vmem((blocks, NBR, BLK, 2 * BLK), bf16),
            vmem((BASIS, local), f32),
            vmem((blocks, 2 * BASIS, 2 * BLK), bf16),
            vmem((3, local, 128), f32),
            vmem((PAD, cell_count), f32),
            vmem((PAD, cell_count), bf16),
            vmem((WIDE, cell_count), bf16),
            vmem((WIDE, cell_count), bf16),
            vmem((blocks, NBR, 2 * EDGE, 2 * BLK), bf16),
            vmem((blocks, WIDE, BLK), bf16),
            vmem((blocks, BLK, WIDE), bf16),
            vmem((blocks, width, BLK), f32),
            vmem((ITERS, width, local), f32),
            vmem((ITERS, 3, EDGE, local), f32),
            vmem((ITERS, regions, TILE, BLK), f32),
            vmem((regions, TILE, BLK), f32),
            vmem((regions, TILE, BLK), f32),
            vmem((ITERS, regions, TILE, BLK), f32),
            vmem((ITERS, regions, TILE, BLK), f32),
            vmem((ITERS, MOMENTS, 1, cell_count), f32),
            vmem((ITERS, shards - 1, MOMENTS, 1, cell_count), f32),
            vmem((8, cell_count), f32),
            vmem((local, cell_count), f32),
            vmem((blocks, BASIS, cell_count), f32),
            vmem((blocks, 2 * BASIS, WIDE), bf16),
            vmem((local, cell_count), f32),
            signals((8,)),
            signals((blocks,)),
            signals((ITERS, 3)),
            signals((ITERS, 3)),
            signals((ITERS, 2)),
            signals((ITERS, 2)),
            signals((ITERS, shards - 1)),
            signals((ITERS, shards - 1)),
        ],
        compiler_params=pltpu.CompilerParams(
            collective_id=0, has_side_effects=True, vmem_limit_bytes=56 * 1024 * 1024
        ),
    )(distribution, velocity, weights, points, neighbours, cells, interpolation, inverse)
    return pl.pallas_call(
        hand_on,
        out_shape=jax.ShapeDtypeStruct(value.shape, f32),
        in_specs=[anywhere],
        out_specs=anywhere,
        scratch_shapes=[vmem((local, cell_count), f32), signals((8,)), signals((8,))],
        compiler_params=pltpu.CompilerParams(vmem_limit_bytes=56 * 1024 * 1024),
    )(value)


def solution(mesh):
    regions, shards = mesh.shape["region"], mesh.shape["vel"]

    def local(distribution, velocity, weights, grid_points, neighbours, interface_cells, interpolation, block_inverse):
        return update(
            regions, shards, 8,
            distribution, velocity.transpose(1, 0, 2), weights, grid_points, neighbours.T,
            interface_cells.transpose(1, 0, 2), interpolation, block_inverse,
        )

    placed = (
        P("region", "vel", None),
        P("region", None, "vel"),
        P("region", "vel"),
        P(),
        P(),
        P("region", None, None),
        P("region", None, "vel", None),
        P("region", "vel", None, None),
    )
    return jax.shard_map(
        local, mesh=mesh, in_specs=placed, out_specs=P("region", "vel", None), check_vma=False
    )
```

```python
import functools
import math

import jax
import jax.numpy as jnp
from jax import lax
from jax.experimental import pallas as pl
from jax.experimental.pallas import tpu as pltpu
from jax.sharding import PartitionSpec as P

VMAX = 8192
BLK = 128
EDGE = 16
NBR = 5
ITERS = 2
PAD = 128
WIDE = 256
BASIS = 16
MOMENTS = 13
TILE = 8

relax_step = 0.5
inflow_step = 0.5
viscous_conductive_ratio = 2.0 / 3.0

MESH = pl.DeviceIdType.MESH
f32 = jnp.float32
bf16 = jnp.bfloat16


def far_first(regions):
    side = math.isqrt(regions // 2)

    def hops(offset):
        total = 0
        for region in range(regions):
            here, there = region // 2, (region + offset) % regions // 2
            for a, b in ((here // side, there // side), (here % side, there % side)):
                total += min((a - b) % side, (b - a) % side)
        return total

    return sorted(range(1, regions), key=lambda offset: (-hops(offset), offset))


def across(a, b):
    return lax.dot_general(a, b, (((1,), (1,)), ((), ())), preferred_element_type=f32)


def plain(a, b):
    return jnp.dot(a, b, preferred_element_type=f32)


def halves(x):
    high = x.astype(bf16)
    return high, (x - high.astype(f32)).astype(bf16)


def moment_rows(x, y, z):
    speed_sq = x * x + y * y + z * z
    return [
        jnp.ones_like(x), x, y, z,
        x * x, y * y, z * z,
        x * y, x * z, y * z,
        x * speed_sq, y * speed_sq, z * speed_sq,
    ]


def cell_rows(m):
    density = m[0]
    over = 1.0 / density
    u, v, w = m[1] * over, m[2] * over, m[3] * over
    energy = m[4] + m[5] + m[6]
    flow_sq = u * u + v * v + w * w
    warmth = (energy * over - flow_sq) / 3.0
    stress_x = m[4] * u + m[7] * v + m[8] * w
    stress_y = m[7] * u + m[5] * v + m[9] * w
    stress_z = m[8] * u + m[9] * v + m[6] * w
    drift = 2.0 * density * flow_sq
    heat_x = 0.5 * (m[10] - 2.0 * stress_x - u * energy + drift * u)
    heat_y = 0.5 * (m[11] - 2.0 * stress_y - v * energy + drift * v)
    heat_z = 0.5 * (m[12] - 2.0 * stress_z - w * energy + drift * w)
    hot = 2.0 * math.pi * warmth
    front = relax_step * density / (hot * jnp.sqrt(hot))
    fall = -0.5 / warmth
    skew = (-2.0 * (1.0 - viscous_conductive_ratio)) / (5.0 * density * warmth * warmth)
    return [front, u, v, w, fall, heat_x * skew, heat_y * skew, heat_z * skew]


def kernel(
    regions, shards, unroll,
    dist_hbm, vel_hbm, weights_hbm, points_hbm, neighbours_hbm, cells_hbm, interp_hbm, inv_hbm, out_hbm,
    points, neighbours, cells, dist, vel, weights, interp, inv, both_inv, both_edge, edge_edge, inv_edge, mats,
    basis_f, basis, columns, onehot_f, onehot, halved, spread, pieces, flow_t, flow, kept, sent, recv, tiles, hold_a, hold_b, moved, reached, part, gathered, coef, rhs, held, falls, out,
    in_sem, out_sem, edge_send, edge_recv, hop_send, hop_recv, part_send, part_recv,
):
    region = lax.axis_index("region")
    shard = lax.axis_index("vel")
    local, cell_count = dist.shape
    blocks = local // BLK
    width = NBR * EDGE

    def shifted(offset):
        return lax.rem(region + offset + regions, regions)

    steps = sorted(range(1, shards), key=lambda step: -min(step, shards - step))
    peers = [lax.rem(shard + step, shards) for step in steps]
    offsets = far_first(regions)
    barrier = pltpu.get_barrier_semaphore()

    def others(body):
        for offset in offsets:
            body(shifted(offset))

    for peer in peers:
        pl.semaphore_signal(barrier, inc=1, device_id=(region, peer), device_id_type=MESH)
    others(lambda r: pl.semaphore_signal(barrier, inc=1, device_id=(r, shard), device_id_type=MESH))

    loads = [
        pltpu.make_async_copy(source, target, in_sem.at[i])
        for i, (source, target) in enumerate(
            [
                (dist_hbm.at[0], dist),
                (vel_hbm, vel),
                (weights_hbm, weights),
                (inv_hbm.at[0], inv),
                (interp_hbm.at[0], interp),
                (cells_hbm, cells),
                (points_hbm, points),
                (neighbours_hbm, neighbours),
            ]
        )
    ]
    for i in (5, 6, 0, 7, 1, 2):
        loads[i].start()

    def remote(source, target, send, arrive, device):
        return pltpu.make_async_remote_copy(
            src_ref=source, dst_ref=target, send_sem=send, recv_sem=arrive, device_id=device, device_id_type=MESH
        )

    def slot_rows(k):
        return pl.ds(EDGE * k, EDGE)

    direct_copies = [
        [
            remote(
                sent.at[turn, slot_rows(k)], recv.at[turn, j], edge_send.at[turn, j], edge_recv.at[turn, j],
                (shifted(offset), shard),
            )
            for j, (k, offset) in enumerate(((1, -1), (0, 1), (4, regions // 2)))
        ]
        for turn in range(ITERS)
    ]
    hold = (hold_a, hold_b)

    def out_copy(turn, r):
        return remote(tiles.at[turn, r], hold[turn].at[region], hop_send.at[turn, 0], hop_recv.at[turn, 0], (r, shard))

    def on_copy(turn, r):
        return remote(moved.at[turn, r], reached.at[turn, region], hop_send.at[turn, 1], hop_recv.at[turn, 1], (r, shard))

    def all_tiles(turn, step):
        ref = (hold[turn] if step == 0 else reached.at[turn]).at[pl.ds(0, regions - 1)]
        return remote(ref, ref, hop_send.at[turn, step], hop_recv.at[turn, step], (shifted(1), shard))

    part_copies = [
        [
            remote(part.at[turn], gathered.at[turn, j], part_send.at[turn, j], part_recv.at[turn, j], (region, peers[j]))
            for j in range(shards - 1)
        ]
        for turn in range(ITERS)
    ]

    def backward():
        stride = lax.rem(neighbours[2, 0] + regions, regions)
        return jnp.where(region < regions // 2, regions - stride, stride)

    def alive(n):
        return jnp.where((shard * blocks + n) * BLK < points[region], f32(1.0), f32(0.0))

    def rows_of(n):
        return pl.ds(pl.multiple_of(n * BLK, BLK), BLK)

    def each(body, init=0):
        return lax.fori_loop(0, blocks, body, init, unroll=unroll)

    def post_edges(turn, n, edges):
        sent[turn, :, rows_of(n)] = edges
        for group in range(regions // blocks):
            start = 2 * EDGE + TILE * group
            tiles[turn, group * blocks + n] = edges[start : start + TILE]

    def send_edges(turn):
        hold[turn][region] = tiles[turn, region]
        others(lambda r: out_copy(turn, r).start())
        for copy in direct_copies[turn]:
            copy.start()

    def send_part(turn, total_part):
        for i in range(MOMENTS):
            part[turn, i] = total_part[i : i + 1, :]
        for copy in part_copies[turn]:
            copy.start()

    with jax.named_scope("onehot"):
        loads[5].wait()
        onehot_f[...] = jnp.zeros_like(onehot_f)
        lane = lax.broadcasted_iota(jnp.int32, (1, cell_count), 1)
        for k in range(NBR):
            for i in range(EDGE):
                row = EDGE * k + i
                onehot_f[row : row + 1, :] = (lane == cells[k, 0, i]).astype(f32)
        picks = onehot_f[...]
        onehot[...] = picks.astype(bf16)
        half = (inflow_step * picks[0:width]).astype(bf16)
        halved[3 * width :, :] = jnp.zeros((WIDE - 3 * width, cell_count), bf16)
        spread[2 * width :, :] = jnp.zeros((WIDE - 2 * width, cell_count), bf16)
        for i in range(2):
            spread[i * width : (i + 1) * width, :] = half
        for i in range(3):
            halved[i * width : (i + 1) * width, :] = half

    with jax.named_scope("wait_dist"):
        loads[6].wait()
        loads[0].wait()
        loads[3].start()
        loads[4].start()

    def first_edges(n, carry):
        high, low = halves(dist[rows_of(n), :] * alive(n))
        pick = onehot[0:width]
        twice = jnp.concatenate([pick, pick], axis=1)
        post_edges(0, n, across(twice, jnp.concatenate([high, low], axis=1)))
        return carry

    with jax.named_scope("first_edges"):
        each(first_edges)

    with jax.named_scope("entry"):
        pl.semaphore_wait(barrier, regions + shards - 2)
        send_edges(0)

    with jax.named_scope("basis"):
        loads[1].wait()
        loads[2].wait()
        loads[7].wait()
        total = points[region]
        x, y, z = vel[0], vel[1], vel[2]
        place = shard * local + lax.broadcasted_iota(jnp.int32, (1, local), 1)
        scale = f32(VMAX) / jnp.full((1, local), total.astype(f32))
        quad = weights[...] * scale * (place < total).astype(f32)
        basis_f[...] = jnp.zeros_like(basis_f)
        for i, row in enumerate(moment_rows(x, y, z)):
            basis_f[i : i + 1, :] = row * quad

        def split_basis(n, carry):
            high, low = halves(basis_f[:, rows_of(n)])
            basis[n, 0:BASIS, 0:BLK] = high
            basis[n, 0:BASIS, BLK : 2 * BLK] = high
            basis[n, BASIS : 2 * BASIS, 0:BLK] = low
            basis[n, BASIS : 2 * BASIS, BLK : 2 * BLK] = jnp.zeros_like(low)
            return carry

        each(split_basis)

    def weighted(n, high, low):
        both = plain(basis[n], jnp.concatenate([high, low], axis=0))
        return both[:BASIS] + both[BASIS:]

    def first_moments(n, acc):
        high, low = halves(dist[rows_of(n), :] * alive(n))
        return acc + weighted(n, high, low)

    with jax.named_scope("first_moments"):
        send_part(0, each(first_moments, jnp.zeros((BASIS, cell_count), f32)))

    with jax.named_scope("turn_columns"):
        basis_f[0:3, :] = jnp.concatenate([x, y, z], axis=0)

        def turn_columns(n, carry):
            turned = jnp.transpose(basis_f[0:8, rows_of(n)])
            for axis in range(3):
                columns[axis, rows_of(n), :] = jnp.broadcast_to(turned[:, axis : axis + 1], (BLK, 128))
            return carry

        each(turn_columns)
        pieces[...] = jnp.zeros_like(pieces)
        flow_t[...] = jnp.zeros_like(flow_t)

    def forward(turn):
        all_tiles(turn, 0).wait_recv()

        back = backward()

        def take(r, carry):
            moved[turn, r] = hold[turn][lax.rem(r + back, regions)]
            return carry

        lax.fori_loop(0, regions, take, 0, unroll=8)
        reached[turn, region] = moved[turn, region]
        others(lambda r: on_copy(turn, r).start())

    def prepare_inv(n, carry):
        high, low = halves(inv[n])
        both_inv[n, :, 0:cell_count] = high
        both_inv[n, :, cell_count : 2 * cell_count] = low
        edges = plain(onehot[0:width], jnp.concatenate([high, low], axis=1)).astype(bf16)
        both_edge[n, 0:width, 0:cell_count] = edges[:, 0:cell_count]
        both_edge[n, 0:width, cell_count : 2 * cell_count] = edges[:, 0:cell_count]
        both_edge[n, width : 2 * width, 0:cell_count] = edges[:, cell_count : 2 * cell_count]
        both_edge[n, width : 2 * width, cell_count : 2 * cell_count] = jnp.zeros((width, cell_count), bf16)
        return carry

    def prepare_edge_edge(group, carry):
        rows = both_edge[pl.ds(2 * group, 2), :, 0:cell_count].reshape(4 * width, cell_count)
        value = across(rows, halved[...])
        lane = lax.broadcasted_iota(jnp.int32, (width, WIDE), 1)
        for i in range(2):
            near = value[2 * i * width : (2 * i + 1) * width]
            fine = value[(2 * i + 1) * width : (2 * i + 2) * width]
            edge_edge[2 * group + i] = jnp.where(lane < 2 * width, near, fine).astype(bf16)
        return carry

    def prepare_inv_edge(n, carry):
        back_h = across(halved[0:width], both_inv[n, :, 0:cell_count]).astype(bf16)
        inv_edge[n, 0:width] = back_h
        inv_edge[n, width : 2 * width] = back_h
        inv_edge[n, 2 * width : WIDE] = across(
            halved[2 * width : WIDE], both_inv[n, :, cell_count : 2 * cell_count]
        ).astype(bf16)
        return carry

    def prepare_mat(n, carry):
        for k in range(NBR):
            high, low = halves(interp[k, rows_of(n), :])
            mats[n, k, :, 0:BLK] = high
            mats[n, k, :, BLK : 2 * BLK] = low
        return carry

    with jax.named_scope("prepare_inv"):
        loads[3].wait()
        each(prepare_inv)
        lax.fori_loop(0, blocks // 2, prepare_edge_edge, 0, unroll=unroll)
    with jax.named_scope("prepare_mat"):
        loads[4].wait()
        each(prepare_mat)
    with jax.named_scope("forward0"):
        forward(0)

    def collect(turn):
        for copy in part_copies[turn]:
            copy.wait_recv()
        moments = part[turn]
        for j in range(shards - 1):
            moments = moments + gathered[turn, j]
        rows = cell_rows([moments[i] for i in range(MOMENTS)])
        for i, row in enumerate(rows):
            coef[i : i + 1, :] = row

    def relax(n, carry):
        on = alive(n)
        chunk = 32
        for tile in range(cell_count // 128):
            lanes = pl.ds(128 * tile, 128)
            front, u, v, w, fall, skew_x, skew_y, skew_z = [coef[i : i + 1, lanes] for i in range(8)]
            for c in range(BLK // chunk):
                rows = pl.ds(pl.multiple_of(n * BLK + c * chunk, chunk), chunk)
                e_x = columns[0, rows, :] - u
                e_y = columns[1, rows, :] - v
                e_z = columns[2, rows, :] - w
                power = (e_x * e_x + e_y * e_y + e_z * e_z) * fall
                lean = e_x * skew_x + e_y * skew_y + e_z * skew_z
                value = front * jnp.exp(power) * (1.0 + lean * (power + 2.5))
                rhs[rows, lanes] = dist[rows, lanes] * on + value
        return carry

    def place_in(k, value):
        high, low = halves(value)
        for n in range(blocks):
            lanes = slice(BLK * n, BLK * (n + 1))
            pieces[n, k, 0:EDGE, 0:BLK] = high[:, lanes]
            pieces[n, k, 0:EDGE, BLK : 2 * BLK] = high[:, lanes]
            pieces[n, k, EDGE : 2 * EDGE, 0:BLK] = low[:, lanes]

    def interpolate(interfaces, done):
        def one(n, carry):
            for k in interfaces:
                both = across(pieces[n, k], mats[n, k])
                high, low = halves(both[:EDGE] + both[EDGE:])
                flow_t[n, EDGE * k : EDGE * (k + 1)] = high
                flow_t[n, width + EDGE * k : width + EDGE * (k + 1)] = low
                flow_t[n, 2 * width + EDGE * k : 2 * width + EDGE * (k + 1)] = high
            if done:
                flow[n] = jnp.transpose(flow_t[n])
            return carry

        each(one)

    def arrive_direct(turn):
        for j, k in enumerate((0, 1, 4)):
            direct_copies[turn][j].wait_recv()
            place_in(k, recv[turn, j])
        interpolate((0, 1, 4), False)

    def arrive(turn):
        all_tiles(turn, 1).wait_recv()
        for k, first in ((3, 0), (2, 2 * blocks)):
            rows = [[reached[turn, first + g * blocks + n] for n in range(blocks)] for g in range(2)]
            place_in(k, jnp.concatenate([jnp.concatenate(r, axis=1) for r in rows], axis=0))

    with jax.named_scope("direct0"):
        arrive_direct(0)
    with jax.named_scope("collect0"):
        collect(0)
    with jax.named_scope("relax0"):
        each(relax)

    def main_edges(n, carry):
        high, low = halves(rhs[rows_of(n), :])
        edges = across(both_edge[n], jnp.concatenate([high, low], axis=1))
        kept[n] = edges[:width] + edges[width:]
        return carry

    def main_moments(n, carry):
        high, low = halves(rhs[rows_of(n), :])
        held[n] = weighted(n, high, low)
        return carry

    with jax.named_scope("main_edges"):
        each(main_edges)
    with jax.named_scope("main_moments"):
        each(main_moments)
    with jax.named_scope("inv_edge0"):
        lax.fori_loop(0, blocks // 2, prepare_inv_edge, 0, unroll=unroll)
    with jax.named_scope("arrive0"):
        arrive(0)
    with jax.named_scope("interpolate0"):
        interpolate((2, 3), False)

    def landed_edges(n, carry):
        post_edges(1, n, (kept[n] + plain(edge_edge[n], flow_t[n])) * alive(n))
        return carry

    def fall_moments(n, carry):
        both = plain(basis[n, :, 0:BLK], jnp.transpose(flow_t[n]))
        fall_h, fall_l = halves(both[:BASIS] + both[BASIS:])
        falls[n, 0:BASIS] = fall_h
        falls[n, BASIS : 2 * BASIS] = fall_l
        return carry

    def landed_moments():
        each(fall_moments)
        spreads = plain(falls[...].reshape(2 * BASIS * blocks, WIDE), spread[...])
        acc = jnp.zeros((BASIS, cell_count), f32)
        for n in range(blocks):
            start = 2 * BASIS * n
            both = spreads[start : start + BASIS] + spreads[start + BASIS : start + 2 * BASIS]
            held_h, held_l = halves(held[n] + both)
            both = across(
                jnp.concatenate(
                    [
                        jnp.concatenate([held_h, held_h], axis=1),
                        jnp.concatenate([held_l, jnp.zeros_like(held_l)], axis=1),
                    ],
                    axis=0,
                ),
                both_inv[n],
            )
            acc = acc + both[:BASIS] + both[BASIS:]
        return acc

    with jax.named_scope("landed_edges"):
        each(landed_edges)
        send_edges(1)
    with jax.named_scope("landed_moments"):
        send_part(1, landed_moments())
    with jax.named_scope("inv_edge1"):
        lax.fori_loop(blocks // 2, blocks, prepare_inv_edge, 0, unroll=unroll)
    with jax.named_scope("forward1"):
        forward(1)
    with jax.named_scope("direct1"):
        arrive_direct(1)
    with jax.named_scope("collect1"):
        collect(1)
    with jax.named_scope("relax1"):
        each(relax)

    def main_result(n, carry):
        high, low = halves(rhs[rows_of(n), :])
        wide = jnp.concatenate(
            [
                jnp.concatenate([high, high], axis=1),
                jnp.concatenate([low, jnp.zeros_like(low)], axis=1),
            ],
            axis=0,
        )
        turned = across(both_inv[n], wide)
        out[rows_of(n), :] = jnp.transpose(turned[:, :BLK] + turned[:, BLK:])
        return carry

    def last(n, carry):
        out[rows_of(n), :] = (out[rows_of(n), :] + plain(flow[n], inv_edge[n])) * alive(n)
        pltpu.make_async_copy(out.at[rows_of(n)], out_hbm.at[0, rows_of(n)], out_sem.at[n]).start()
        return carry

    with jax.named_scope("main_result"):
        each(main_result)
    with jax.named_scope("arrive1"):
        arrive(1)
    with jax.named_scope("interpolate1"):
        interpolate((2, 3), True)
    with jax.named_scope("last"):
        each(last)
    with jax.named_scope("finish"):
        for n in range(blocks):
            pltpu.make_async_copy(out.at[rows_of(n)], out_hbm.at[0, rows_of(n)], out_sem.at[n]).wait()
        for turn in range(ITERS):
            for copy in part_copies[turn] + direct_copies[turn]:
                copy.wait_send()
            for step in range(2):
                all_tiles(turn, step).wait_send()


def hand_on(value_hbm, out_hbm, held, in_sems, out_sems):
    parts = in_sems.shape[0]
    rows = held.shape[0] // parts
    ways = [pl.ds(i * rows, rows) for i in range(parts)]
    takes = [pltpu.make_async_copy(value_hbm.at[0, way], held.at[way], in_sems.at[i]) for i, way in enumerate(ways)]
    gives = [pltpu.make_async_copy(held.at[way], out_hbm.at[0, way], out_sems.at[i]) for i, way in enumerate(ways)]
    for take in takes:
        take.start()
    for take, give in zip(takes, gives):
        take.wait()
        give.start()
    for give in gives:
        give.wait()


def update(regions, shards, unroll, *arrays):
    distribution, velocity, weights, points, neighbours, cells, interpolation, inverse = arrays
    local, cell_count = distribution.shape[1:]
    blocks = local // BLK
    width = NBR * EDGE
    anywhere = pl.BlockSpec(memory_space=pl.ANY)
    vmem = pltpu.VMEM
    signals = pltpu.SemaphoreType.DMA
    value = pl.pallas_call(
        functools.partial(kernel, regions, shards, unroll),
        out_shape=jax.ShapeDtypeStruct((1, local, cell_count), f32),
        in_specs=[anywhere] * 8,
        out_specs=anywhere,
        scratch_shapes=[
            pltpu.SMEM(points.shape, jnp.int32),
            pltpu.SMEM(neighbours.shape, jnp.int32),
            pltpu.SMEM(cells.shape, jnp.int32),
            vmem((local, cell_count), f32),
            vmem((3, 1, local), f32),
            vmem((1, local), f32),
            vmem((NBR, local, BLK), f32),
            vmem((blocks, cell_count, cell_count), f32),
            vmem((blocks, cell_count, 2 * cell_count), bf16),
            vmem((blocks, 2 * width, 2 * cell_count), bf16),
            vmem((blocks, width, WIDE), bf16),
            vmem((blocks, WIDE, cell_count), bf16),
            vmem((blocks, NBR, BLK, 2 * BLK), bf16),
            vmem((BASIS, local), f32),
            vmem((blocks, 2 * BASIS, 2 * BLK), bf16),
            vmem((3, local, 128), f32),
            vmem((PAD, cell_count), f32),
            vmem((PAD, cell_count), bf16),
            vmem((WIDE, cell_count), bf16),
            vmem((WIDE, cell_count), bf16),
            vmem((blocks, NBR, 2 * EDGE, 2 * BLK), bf16),
            vmem((blocks, WIDE, BLK), bf16),
            vmem((blocks, BLK, WIDE), bf16),
            vmem((blocks, width, BLK), f32),
            vmem((ITERS, width, local), f32),
            vmem((ITERS, 3, EDGE, local), f32),
            vmem((ITERS, regions, TILE, BLK), f32),
            vmem((regions, TILE, BLK), f32),
            vmem((regions, TILE, BLK), f32),
            vmem((ITERS, regions, TILE, BLK), f32),
            vmem((ITERS, regions, TILE, BLK), f32),
            vmem((ITERS, MOMENTS, 1, cell_count), f32),
            vmem((ITERS, shards - 1, MOMENTS, 1, cell_count), f32),
            vmem((8, cell_count), f32),
            vmem((local, cell_count), f32),
            vmem((blocks, BASIS, cell_count), f32),
            vmem((blocks, 2 * BASIS, WIDE), bf16),
            vmem((local, cell_count), f32),
            signals((8,)),
            signals((blocks,)),
            signals((ITERS, 3)),
            signals((ITERS, 3)),
            signals((ITERS, 2)),
            signals((ITERS, 2)),
            signals((ITERS, shards - 1)),
            signals((ITERS, shards - 1)),
        ],
        compiler_params=pltpu.CompilerParams(
            collective_id=0, has_side_effects=True, vmem_limit_bytes=56 * 1024 * 1024
        ),
    )(distribution, velocity, weights, points, neighbours, cells, interpolation, inverse)
    return pl.pallas_call(
        hand_on,
        out_shape=jax.ShapeDtypeStruct(value.shape, f32),
        in_specs=[anywhere],
        out_specs=anywhere,
        scratch_shapes=[vmem((local, cell_count), f32), signals((8,)), signals((8,))],
        compiler_params=pltpu.CompilerParams(vmem_limit_bytes=56 * 1024 * 1024),
    )(value)


def solution(mesh):
    regions, shards = mesh.shape["region"], mesh.shape["vel"]

    def local(distribution, velocity, weights, grid_points, neighbours, interface_cells, interpolation, block_inverse):
        return update(
            regions, shards, 8,
            distribution, velocity.transpose(1, 0, 2), weights, grid_points, neighbours.T,
            interface_cells.transpose(1, 0, 2), interpolation, block_inverse,
        )

    placed = (
        P("region", "vel", None),
        P("region", None, "vel"),
        P("region", "vel"),
        P(),
        P(),
        P("region", None, None),
        P("region", None, "vel", None),
        P("region", "vel", None, None),
    )
    return jax.shard_map(
        local, mesh=mesh, in_specs=placed, out_specs=P("region", "vel", None), check_vma=False
    )
```
